128 devices in a mesh: band: 4 (over y), strip: 32 (over x, z, core).
Axes of the slice: x: 4, y: 4, z: 4, core: 2. Of those that a mesh axis runs over, the one named last changes fastest.
Arguments:
- cloud_field: bfloat16 [256, 1024, 512], P('band', 'strip'), may hold values from -6 to 6
- row_gain: float32 [512], replicated, may hold values from 0.1 to 1.9
- row_qkv: bfloat16 [512, 1536], replicated, may hold values from -0.25 to 0.25
- row_out: bfloat16 [512, 512], replicated, may hold values from -1 to 1
- col_gain: float32 [512], replicated, may hold values from 0.1 to 1.9
- col_qkv: bfloat16 [512, 1536], replicated, may hold values from -0.25 to 0.25
- col_out: bfloat16 [512, 512], replicated, may hold values from -1 to 1
- plant_cell: int32 [16384], P(('band', 'strip')), may hold values from 0 to 2047
- plant_decoder_device: int32 [16384, 1], P(('band', 'strip')), may hold values from 0 to 127; in each aligned block of 128 rows (0 to 127, 128 to 255, ...) at most 2 rows name the same one
- plant_capacity: int32 [16384], P(('band', 'strip')), may hold values from 100 to 5000
- decode_first: bfloat16 [65536, 512], P(('band', 'strip')), may hold values from -0.25 to 0.25
- decode_second: bfloat16 [128, 512], P(('band', 'strip')), may hold values from -0.25 to 0.25
Outputs:
- final_field: bfloat16 [256, 1024, 512], P('band', 'strip')
- plant_power: float32 [16384], P(('band', 'strip'))
- fleet_yield: float32 [], replicated
The draws below stay inside these ranges and needn't reach their ends.
Inputs may be any that keep to these rules, and one draw needn't show every extreme that they name: `plant_decoder_device`: among the 128 plants listed on one device, no owner is named more than 2 times.
All inputs are finite; a program needn't handle non-finite values.
Results may differ from the reference program's by a relative error of at most 0.015.
Values may be sent and summed in bfloat16 or wider, within the bound.
No kernel may reach another device: no remote copies, remote signals or barrier semaphores. Data moves between devices by JAX's collectives and lax.ppermute only.
A program may use at most 64 MiB of HBM per device.

```python
import math
import jax
import jax.numpy as jnp
import numpy as np
from jax import lax

D = 512
HEADS = 8
DEC = 512
ROWS_DEV = 64
COLS_DEV = 32
PLANT_DEV = 128
TOK_DEV = 2048
H = 256
W = 1024
OWNERS = 128
MOST = 2
PLANTS = 16384
N_STRIP = 32


def draw_plant_capacity(key, part):
    base = jax.random.randint(key, (PLANTS,), 100, 1001).astype(jnp.int32)
    device_of = jnp.arange(PLANTS, dtype=jnp.int32) // PLANT_DEV
    factor = (OWNERS + 4 * device_of).astype(jnp.int32)
    return (base * factor // OWNERS).astype(jnp.int32)


def touch_ends(values, stream_key, smallest, top_value):
    index_at = [jax.random.randint(jax.random.fold_in(stream_key, axis), (), 0, length) for axis, length in enumerate(values.shape)]
    main_axis = values.shape.index(max(values.shape))
    neighbour = index_at[:main_axis] + [(index_at[main_axis] + 1) % values.shape[main_axis]] + index_at[main_axis + 1:]
    return values.at[tuple(index_at)].set(smallest).at[tuple(neighbour)].set(top_value)


def shard_levels(rng, extent, pieces, smallest, largest):
    factor_of = 1.0
    for position, blocks in pieces:
        draws = jax.random.uniform(jax.random.fold_in(jax.random.fold_in(rng, 6), position), (blocks,), jnp.float32, smallest / len(pieces), largest / len(pieces))
        factor_of = factor_of * jnp.repeat(jnp.exp(draws), extent[position] // blocks).reshape((-1,) + (1,) * (len(extent) - 1 - position))
    return factor_of


def assign_block(own_key, own, number, rows, number_of, top, reach, slope):
    order = jax.random.permutation(own_key, number_of)
    packed, ordinary = shares(number_of, rows * top, reach, slope, True), shares(number_of, rows * top, reach, slope, False)
    places = jnp.arange(number_of)

    def named(tallies, turn):
        used = int((tallies > 0).sum())
        fixed = max(1, used // 4)
        passed = fixed + (places - fixed + turn * (used - fixed)) % max(1, number_of - fixed)
        return jnp.zeros((number_of,), jnp.int32).at[order[jnp.where(places < fixed, places, passed)]].set(jnp.asarray(tallies, jnp.int32))

    tallies = jnp.where(number % 4 == 0, named(packed, number // 4), named(ordinary, number - number // 4 - 1))
    mixed = jax.random.permutation(jax.random.fold_in(own, 3), number_of)
    donor, receiver = mixed[0:number_of // 2 * 2:2], mixed[1:number_of // 2 * 2:2]
    margin = jnp.minimum(tallies[donor] - 1, reach - tallies[receiver]) // 2
    margin = jnp.where((donor == order[0]) | (receiver == order[0]) | (tallies[receiver] == 0), 0, jnp.maximum(margin, 0))
    passed = jax.random.randint(jax.random.fold_in(own, 4), (number_of // 2,), 0, 1 << 20) % (margin + 1)
    tallies = tallies.at[donor].add(-passed).at[receiver].add(passed)
    labels = jnp.searchsorted(jnp.cumsum(tallies), jnp.arange(rows * top), side="right").astype(jnp.int32)
    table = labels.reshape(top, rows).T
    table = table[jax.random.permutation(jax.random.fold_in(own, 1), rows)]
    turn = jax.random.randint(jax.random.fold_in(own, 2), (rows, 1), 0, top)
    return jnp.take_along_axis(table, (jnp.arange(top)[None, :] + turn) % top, axis=1)


def shares(count, total, bound, slope, full):
    portions = [(1 << 20) // math.isqrt(grade ** slope) + 1 for grade in range(1, count + 1)]
    largest = bound if full else min(bound, max(-(-total // count), total * portions[0] // sum(portions)))
    least = 1 if total - largest >= count - 1 else 0
    given, spare = [largest] + [least] * (count - 1), total - largest - least * (count - 1)
    while spare > 0:
        movable = [i for i in range(1, count) if given[i] < largest] or [i for i in range(1, count) if given[i] < bound]
        whole, left = sum([portions[i] for i in movable]), spare
        for i in movable:
            extra = min(bound - given[i], max(1, left * portions[i] // whole), spare)
            given[i] = given[i] + extra
            spare = spare - extra
    return np.array(given)


def normal_values(own_key, shape, scale, most, split=(), kind=jnp.bfloat16):
    drawn = jax.random.normal(own_key, shape, jnp.float32) * scale
    if len(split) > 0:
        drawn = shard_levels(own_key, shape, split, -0.22, 0.18) * drawn
    return jnp.clip(drawn, min=-most, max=most).astype(kind)


def setup_inputs(seed: int = 0) -> dict:
    key_list = jax.random.split(jax.random.key(seed), 13)
    cloud_field = normal_values(key_list[0], (H, W, D), 1.0, 6.0, ((0, 4), (1, 32)))
    row_gain = jnp.clip(1.0 + 0.18 * jax.random.normal(key_list[1], (D,), jnp.float32), 0.1, 1.9)
    row_qkv = normal_values(key_list[2], (D, 3 * D), D ** -0.5, 0.25)
    row_out = normal_values(key_list[3], (D, D), (D // 16) ** -0.5, 1.0)
    col_gain = jnp.clip(1.0 + 0.18 * jax.random.normal(key_list[4], (D,), jnp.float32), 0.1, 1.9)
    col_qkv = normal_values(key_list[5], (D, 3 * D), D ** -0.5, 0.25)
    col_out = normal_values(key_list[6], (D, D), (D // 16) ** -0.5, 1.0)
    plant_cell = touch_ends(jax.random.randint(key_list[7], (PLANTS,), 0, TOK_DEV), jax.random.fold_in(key_list[7], 1), 0, TOK_DEV - 1).astype(jnp.int32)
    plant_decoder_device_keys = jax.random.split(jax.random.fold_in(key_list[8], 1), PLANTS // PLANT_DEV)
    plant_decoder_device_turns = jax.random.permutation(jax.random.fold_in(key_list[8], 3), PLANTS // PLANT_DEV)
    plant_decoder_device = jax.vmap(lambda own, number: assign_block(jax.random.fold_in(key_list[8], 2), own, number, PLANT_DEV, OWNERS, 1, MOST, 2))(plant_decoder_device_keys, plant_decoder_device_turns).reshape((PLANTS, 1))
    plant_capacity = draw_plant_capacity(jax.random.fold_in(key_list[12], 71), 0)
    decode_first = normal_values(key_list[10], (OWNERS * D, DEC), D ** -0.5, 0.25, ((0, 128),))
    decode_second = normal_values(key_list[11], (OWNERS, DEC), DEC ** -0.5, 0.25, ((0, 128),))
    return dict(cloud_field=cloud_field, row_gain=row_gain, row_qkv=row_qkv, row_out=row_out, col_gain=col_gain, col_qkv=col_qkv, col_out=col_out, plant_cell=plant_cell, plant_decoder_device=plant_decoder_device, plant_capacity=plant_capacity, decode_first=decode_first, decode_second=decode_second)


EPS = 1e-06
TAU = 12.0

def norm_rows(values, scale_factor):
    widened = values.astype(jnp.float32)
    return widened * lax.rsqrt(lax.optimization_barrier(jnp.mean(widened * widened, axis=-1, keepdims=True)) + EPS) * scale_factor.astype(jnp.float32)

def heads_norm(values):
    leading = values.shape[:-1]
    split_up = values.reshape(leading + (HEADS, values.shape[-1] // HEADS))
    normed = split_up * lax.rsqrt(lax.optimization_barrier(jnp.mean(split_up * split_up, axis=-1, keepdims=True)) + EPS)
    return normed.reshape(values.shape)

def project(tokens_in, scale_factor, weight_qkv):
    leading = tokens_in.shape[:-1]
    model_width = tokens_in.shape[-1]
    head_width = model_width // HEADS
    normed = norm_rows(tokens_in, scale_factor).astype(jnp.bfloat16).reshape(-1, model_width)
    projected = jnp.dot(normed, weight_qkv, preferred_element_type=jnp.float32)
    query = heads_norm(projected[:, :model_width]) * (TAU / head_width)
    keys_part = heads_norm(projected[:, model_width:2 * model_width])
    values_part = projected[:, 2 * model_width:]
    shaped = leading + (model_width,)
    return (query.astype(jnp.bfloat16).reshape(shaped), keys_part.astype(jnp.bfloat16).reshape(shaped), values_part.astype(jnp.bfloat16).reshape(shaped))

def attend(query, keys_part, values_part):
    batch_size, length, model_width = query.shape
    head_width = model_width // HEADS

    def split_heads(tensor):
        return tensor.reshape(batch_size, length, HEADS, head_width).transpose(2, 0, 1, 3)

    def one_head(operands):
        query_rows, key_rows, value_rows = operands
        attention_scores = jnp.einsum('zxe,zle->zxl', query_rows.astype(jnp.float32), key_rows.astype(jnp.float32))
        weights = jnp.exp(attention_scores)
        row_total = lax.optimization_barrier(jnp.sum(weights, axis=-1, keepdims=True))
        weights_bfloat = (weights / row_total).astype(jnp.bfloat16)
        return jnp.einsum('pem,pmj->pej', weights_bfloat.astype(jnp.float32), value_rows.astype(jnp.float32)).astype(jnp.bfloat16)
    context = lax.map(one_head, (split_heads(query), split_heads(keys_part), split_heads(values_part)))
    return context.transpose(1, 2, 0, 3).reshape(batch_size, length, model_width)

def finish(tokens_in, context, weight_out):
    model_width = tokens_in.shape[-1]
    mixed = jnp.dot(context.reshape(-1, model_width), weight_out, preferred_element_type=jnp.float32)
    return (tokens_in.astype(jnp.float32) + mixed.reshape(tokens_in.shape)).astype(jnp.bfloat16)

def mix_layer(tokens_in, scale_factor, weight_qkv, weight_out):
    query, keys_part, values_part = project(tokens_in, scale_factor, weight_qkv)
    return finish(tokens_in, attend(query, keys_part, values_part), weight_out)

def reference(cloud_field, row_gain, row_qkv, row_out, col_gain, col_qkv, col_out, plant_cell, plant_decoder_device, plant_capacity, decode_first, decode_second):
    rows_all, cols_all, model_width = cloud_field.shape
    row_blocks = cloud_field.reshape(rows_all // 8, 8, cols_all, model_width)
    after_rows = lax.map(lambda rows_block: mix_layer(rows_block, row_gain, row_qkv, row_out), row_blocks)
    after_rows = after_rows.reshape(rows_all, cols_all, model_width)
    col_blocks = after_rows.transpose(1, 0, 2).reshape(cols_all // 8, 8, rows_all, model_width)
    after_cols = lax.map(lambda cols_block: mix_layer(cols_block, col_gain, col_qkv, col_out), col_blocks)
    final_field = after_cols.reshape(cols_all, rows_all, model_width).transpose(1, 0, 2)
    device_of = jnp.arange(PLANTS, dtype=jnp.int32) // PLANT_DEV
    band_of = device_of // N_STRIP
    strip_of = device_of % N_STRIP
    row_of = (band_of * ROWS_DEV + plant_cell // COLS_DEV).astype(jnp.int32)
    col_of = (strip_of * COLS_DEV + plant_cell % COLS_DEV).astype(jnp.int32)
    features = final_field[row_of, col_of]
    owners = plant_decoder_device[:, 0]
    owner_grid = owners.reshape(OWNERS, PLANT_DEV)
    one_hot = (owner_grid[:, :, None] == jnp.arange(OWNERS, dtype=jnp.int32)[None, None, :]).astype(jnp.int32)
    running = jnp.cumsum(one_hot, axis=1).astype(jnp.int32)
    slot_of = lax.optimization_barrier(jnp.sum(one_hot * (running - 1), axis=2)).astype(jnp.int32).reshape(PLANTS)
    token_position = (owners * (OWNERS * MOST) + device_of * MOST + slot_of).astype(jnp.int32)
    table = jnp.zeros((OWNERS * OWNERS * MOST, model_width), jnp.bfloat16).at[token_position].set(features)
    table = table.reshape(OWNERS, OWNERS * MOST, model_width)
    first_parts = decode_first.reshape(OWNERS, model_width, DEC)

    def decode_owner(operands):
        slots_in, first_part, second_part = operands
        hidden = jax.nn.gelu(jnp.dot(slots_in, first_part, preferred_element_type=jnp.float32)).astype(jnp.bfloat16)
        return jax.nn.softplus(jnp.dot(hidden.astype(jnp.float32), second_part.astype(jnp.float32)))
    yields = lax.map(decode_owner, (table, first_parts, decode_second)).reshape(-1)
    capacity_w = plant_capacity.astype(jnp.float32) * 0.001
    plant_power = capacity_w * yields[token_position]
    fleet_yield = jnp.sum(plant_power) / float(PLANTS)
    return (final_field, plant_power, fleet_yield)
```

```python
import math

import jax
import jax.numpy as jnp
from jax import lax
from jax.experimental import pallas as pl
from jax.experimental.pallas import tpu as pltpu
from jax.sharding import PartitionSpec as P

HEADS = 8
EPS = 1e-06
TAU = 12.0
BF = jnp.bfloat16
F32 = jnp.float32
LOG2E = math.log2(math.e)
VMEM_LIMIT = 56 * 1024 * 1024


def _dot(a, b):
    return jnp.dot(a, b, preferred_element_type=F32)


def _dot_t(a, b):
    return lax.dot_general(a, b, (((1,), (1,)), ((), ())), preferred_element_type=F32)


def _norm(x, gain):
    return x * lax.rsqrt(jnp.mean(x * x, axis=-1, keepdims=True) + EPS) * gain


def _get(ref, rows):
    return jnp.concatenate([ref[j, rows, :] for j in range(4)], axis=1)


def _put(ref, rows, value):
    for j in range(4):
        ref[j, rows, :] = value[:, 128 * j : 128 * (j + 1)]


def _first_half(shape):
    return lax.broadcasted_iota(jnp.int32, shape, 1) % 128 < 64


def _project(normed, wqkv_ref, seg_ref, rows, q_s, k0_s, k1_s, v0_s, v1_s):
    half = 256
    seg = seg_ref[...]
    even = _first_half((normed.shape[0], half))
    zero = jnp.zeros((normed.shape[0], half), BF)
    one = jnp.ones((normed.shape[0], half), BF)
    for h in range(2):
        lanes = slice(h * half, (h + 1) * half)
        q = _dot(normed, wqkv_ref[:, h * half : (h + 1) * half])
        scale = lax.rsqrt(_dot((q * q).astype(BF), seg) + EPS)
        q_s[rows, lanes] = (q * (scale * (TAU / 64 * LOG2E))).astype(BF)
        k = _dot(normed, wqkv_ref[:, 512 + h * half : 512 + (h + 1) * half])
        scale = lax.rsqrt(_dot((k * k).astype(BF), seg) + EPS)
        k = (k * scale).astype(BF)
        k0_s[rows, lanes] = jnp.where(even, k, zero)
        k1_s[rows, lanes] = jnp.where(even, zero, k)
        v = _dot(normed, wqkv_ref[:, 1024 + h * half : 1024 + (h + 1) * half]).astype(BF)
        v0_s[rows, lanes] = jnp.where(even, v, one)
        v1_s[rows, lanes] = jnp.where(even, one, v)


def _pair(q, k0, k1, v0, v1):
    o0 = _dot(jnp.exp2(_dot_t(q, k0)).astype(BF), v0)
    o1 = _dot(jnp.exp2(_dot_t(q, k1)).astype(BF), v1)
    even = _first_half(o0.shape)
    total = pltpu.roll(jnp.where(even, o1, o0), 64, 1)
    return (jnp.where(even, o0, o1) / total).astype(BF)


def _row_kernel(x_ref, g_ref, wqkv_ref, wo_ref, seg_ref, out_ref, q_s, k0_s, k1_s, v0_s, v1_s, c_s):
    tok, blk = 1024, 256
    gain = g_ref[...]
    for t in range(tok // blk):
        x = x_ref[8 * t : 8 * t + 8, 0].reshape(blk, 512).astype(F32)
        _project(
            _norm(x, gain).astype(BF), wqkv_ref, seg_ref, slice(t * blk, (t + 1) * blk), q_s, k0_s, k1_s, v0_s, v1_s
        )

    def step(i, _):
        lanes = pl.ds(pl.multiple_of(i * 128, 128), 128)
        k0, k1, v0, v1 = k0_s[:, lanes], k1_s[:, lanes], v0_s[:, lanes], v1_s[:, lanes]
        for t in range(tok // blk):
            rows = slice(t * blk, (t + 1) * blk)
            c_s[rows, lanes] = _pair(q_s[rows, lanes], k0, k1, v0, v1)
        return 0

    lax.fori_loop(0, 4, step, 0)
    for t in range(tok // blk):
        x = x_ref[8 * t : 8 * t + 8, 0].reshape(blk, 512).astype(F32)
        y = (x + _dot(c_s[t * blk : (t + 1) * blk, :], wo_ref[...])).astype(BF).reshape(8, 4, 8, 512)
        for b in range(4):
            out_ref[b, 8 * t : 8 * t + 8] = y[:, b]


def row_layer(x, which, gain, wqkv, wo, seg):
    tokens = pltpu.VMEM((1024, 512), BF)
    whole = lambda *shape: pl.BlockSpec(shape, lambda i: (0,) * len(shape))
    return pl.pallas_call(
        _row_kernel,
        grid=(1,),
        out_shape=jax.ShapeDtypeStruct((4, 32, 8, 512), BF),
        in_specs=[
            pl.BlockSpec((32, 1, 32, 512), lambda i: (0, which, 0, 0)),
            whole(1, 512),
            whole(512, 1536),
            whole(512, 512),
            whole(256, 256),
        ],
        out_specs=whole(4, 32, 8, 512),
        scratch_shapes=[tokens] * 6,
        compiler_params=pltpu.CompilerParams(vmem_limit_bytes=VMEM_LIMIT),
        cost_estimate=pl.CostEstimate(flops=12_000_000_000, bytes_accessed=4_000_000, transcendentals=8_000_000),
        name="row_layer",
    )(x, gain, wqkv, wo, seg)


def _col_kernel(
    x0_ref, x1_ref, g_ref, wqkv_ref, wo_ref, seg_ref, idx_ref, y_ref, send_ref,
    wide_s, q_s, k0_s, k1_s, v0_s, v1_s, c_s,
):
    blk = 256
    gain = g_ref[...]
    for r, x_ref in enumerate((x0_ref, x1_ref)):
        for t in range(4):
            x = x_ref[32 * t : 32 * t + 32].reshape(blk, 512).astype(F32)
            _put(wide_s, slice(r * 1024 + t * blk, r * 1024 + (t + 1) * blk), _norm(x, gain))

    def project(c, _):
        normed = _get(wide_s, pl.ds(c, 256, stride=8)).astype(BF)
        rows = pl.ds(pl.multiple_of(c * 256, 256), 256)
        _project(normed, wqkv_ref, seg_ref, rows, q_s, k0_s, k1_s, v0_s, v1_s)
        return 0

    lax.fori_loop(0, 8, project, 0)

    def attend(c, _):
        rows = pl.ds(pl.multiple_of(c * 256, 256), 256)
        for p in range(4):
            lanes = slice(p * 128, (p + 1) * 128)
            c_s[rows, lanes] = _pair(
                q_s[rows, lanes], k0_s[rows, lanes], k1_s[rows, lanes], v0_s[rows, lanes], v1_s[rows, lanes]
            )
        _put(wide_s, pl.ds(c, 256, stride=8), _dot(c_s[rows, :], wo_ref[...]))
        return 0

    lax.fori_loop(0, 8, attend, 0)
    for r, x_ref in enumerate((x0_ref, x1_ref)):
        for t in range(4):
            x = x_ref[32 * t : 32 * t + 32].reshape(blk, 512).astype(F32)
            y = x + _get(wide_s, slice(r * 1024 + t * blk, r * 1024 + (t + 1) * blk))
            y_ref[32 * t : 32 * t + 32, r] = y.astype(BF).reshape(32, 8, 512)
    for b in range(4):
        y = y_ref[32 * b : 32 * b + 32].reshape(512, 512)
        for m in range(2):
            k = 2 * b + m
            pick = lax.broadcasted_iota(jnp.int32, (128, 512), 1) == idx_ref[:, k : k + 1]
            _put(wide_s, pl.ds(k, 128, stride=8), _dot(pick.astype(F32).astype(BF), y))
    send_ref[...] = _get(wide_s, slice(0, 1024)).astype(BF).reshape(128, 8, 512)


def col_layer(x0, x1, gain, wqkv, wo, seg, idx):
    tokens = pltpu.VMEM((2048, 512), BF)
    return pl.pallas_call(
        _col_kernel,
        out_shape=(jax.ShapeDtypeStruct((128, 2, 8, 512), BF), jax.ShapeDtypeStruct((128, 8, 512), BF)),
        in_specs=[pl.BlockSpec(memory_space=pltpu.VMEM)] * 7,
        out_specs=(pl.BlockSpec(memory_space=pltpu.VMEM),) * 2,
        scratch_shapes=[pltpu.VMEM((4, 2048, 128), F32)] + [tokens] * 6,
        compiler_params=pltpu.CompilerParams(vmem_limit_bytes=VMEM_LIMIT),
        cost_estimate=pl.CostEstimate(flops=12_000_000_000, bytes_accessed=9_000_000, transcendentals=4_000_000),
        name="col_layer",
    )(x0, x1, gain, wqkv, wo, seg, idx)


def _decode_kernel(f_ref, w1_ref, w2_ref, cap_ref, out_ref, logit_s):
    w2 = jnp.broadcast_to(w2_ref[...], (128, 512))
    for t in range(4):
        feats = f_ref[32 * t : 32 * t + 32].reshape(256, 512)
        hidden = jax.nn.gelu(_dot(feats, w1_ref[...])).astype(BF)
        logit_s[t * 256 : (t + 1) * 256, :] = _dot_t(hidden, w2)
    lane = lax.broadcasted_iota(jnp.int32, (32, 128), 1)
    power = jnp.zeros((32, 128), F32)
    sums = []
    for k in range(8):
        logit = logit_s[pl.ds(k, 128, stride=8), :]
        cap = cap_ref[:, k : k + 1]
        value = jnp.maximum(logit, 0.0) + jnp.log1p(jnp.exp(-jnp.abs(logit)))
        value = jnp.where(cap > 0, value, 0.0)
        weighted = value * (cap * 0.001)
        fold = lambda a: (a[0:32] + a[32:64]) + (a[64:96] + a[96:128])
        sums.append(fold(value))
        power = power + fold(weighted)
    total = jnp.sum(power, axis=0, keepdims=True)
    for b in range(4):
        rows = jnp.where(lane == 0, sums[2 * b], jnp.where(lane == 1, sums[2 * b + 1], total))
        out_ref[32 * b : 32 * b + 32, :] = rows


def decode(features, w1, w2, caps):
    return pl.pallas_call(
        _decode_kernel,
        out_shape=jax.ShapeDtypeStruct((128, 128), F32),
        scratch_shapes=[pltpu.VMEM((1024, 128), F32)],
        compiler_params=pltpu.CompilerParams(vmem_limit_bytes=VMEM_LIMIT),
        cost_estimate=pl.CostEstimate(flops=600_000_000, bytes_accessed=2_000_000, transcendentals=600_000),
        name="decode",
    )(features, w1, w2, caps)


def _power_kernel(back_ref, owner_ref, slot_ref, cap_ref, power_ref, fleet_ref):
    back = back_ref[...]
    named = lax.broadcasted_iota(jnp.int32, (128, 128), 0) == owner_ref[...]
    first = jnp.sum(jnp.where(named, back[:, 0:1], 0.0), axis=0, keepdims=True)
    second = jnp.sum(jnp.where(named, back[:, 1:2], 0.0), axis=0, keepdims=True)
    value = jnp.where(slot_ref[...] == 0, first, second)
    power_ref[...] = cap_ref[...].astype(F32) * 0.001 * value
    fleet_ref[...] = jnp.sum(back, axis=0, keepdims=True) / 16384.0


def power(back, owner, slot, cap):
    return pl.pallas_call(
        _power_kernel,
        out_shape=(jax.ShapeDtypeStruct((1, 128), F32), jax.ShapeDtypeStruct((1, 128), F32)),
        name="plant_power",
    )(back, owner, slot, cap)


def body(
    cloud_field, row_gain, row_qkv, row_out, col_gain, col_qkv, col_out,
    plant_cell, plant_decoder_device, plant_capacity, decode_first, decode_second,
):
    everyone = ("band", "strip")
    a2a = lambda x, axis: lax.all_to_all(x, axis, split_axis=0, concat_axis=0, tiled=True)
    seg_of = jnp.arange(256) // 64
    seg = jnp.where(seg_of[:, None] == seg_of[None, :], 1.0 / 64, 0.0).astype(BF)
    tokens = a2a(cloud_field.reshape(32, 2, 32, 512), "strip")

    owner = plant_decoder_device[:, 0]
    listed = lax.all_gather(jnp.stack([plant_cell, owner, plant_capacity]), "band")
    cell_all, owner_all, cap_all = listed[:, 0], listed[:, 1], listed[:, 2]
    earlier = jnp.arange(128)[None, :] < jnp.arange(128)[:, None]
    same = (owner_all[:, :, None] == owner_all[:, None, :]) & earlier[None]
    slot_all = jnp.sum(same.astype(jnp.int32), axis=2)
    mine = (cell_all % 32) // 8 == lax.axis_index("band")
    token = jnp.where(mine, (cell_all // 32) * 8 + cell_all % 8, -1)
    there = (owner_all[:, None, :] == jnp.arange(128)[None, :, None])[:, :, None, :] & (
        slot_all[:, None, None, :] == jnp.arange(2)[None, None, :, None]
    )
    there = there & mine[:, None, None, :]
    idx = jnp.sum(jnp.where(there, token[:, None, None, :] + 1, 0), axis=-1) - 1
    caps = jnp.sum(jnp.where(there, cap_all[:, None, None, :], 0), axis=-1).astype(F32)
    idx = idx.transpose(1, 0, 2).reshape(128, 8)
    caps = caps.transpose(1, 0, 2).reshape(128, 8)
    caps = jnp.pad(caps, ((0, 0), (0, 120))).reshape(128, 1, 128)
    caps = a2a(caps, everyone).reshape(128, 128)
    my_same = (owner[:, None] == owner[None, :]) & earlier.T
    my_slot = jnp.sum(my_same.astype(jnp.int32), axis=0)

    row_args = (row_gain.reshape(1, 512), row_qkv, row_out, seg)
    sent0 = a2a(row_layer(tokens, 0, *row_args).reshape(128, 8, 512), everyone)
    sent1 = a2a(row_layer(tokens, 1, *row_args).reshape(128, 8, 512), everyone)
    columns, features = col_layer(sent0, sent1, col_gain.reshape(1, 512), col_qkv, col_out, seg, idx)
    features = a2a(features, everyone)
    field = a2a(columns.reshape(4, 64, 8, 512), "band")
    final_field = field.transpose(1, 0, 2, 3).reshape(64, 32, 512)
    payload = decode(features, decode_first, decode_second, caps)
    back = a2a(payload.reshape(128, 1, 128), everyone).reshape(128, 128)
    plant_power, fleet = power(
        back, owner.reshape(1, 128), my_slot.reshape(1, 128), plant_capacity.reshape(1, 128)
    )
    return (final_field, plant_power.reshape(128), fleet[0, 2])


def solution(mesh):
    return jax.shard_map(
        body,
        mesh=mesh,
        in_specs=(
            P("band", "strip", None),
            P(),
            P(),
            P(),
            P(),
            P(),
            P(),
            P(("band", "strip")),
            P(("band", "strip"), None),
            P(("band", "strip")),
            P(("band", "strip"), None),
            P(("band", "strip"), None),
        ),
        out_specs=(P("band", "strip", None), P(("band", "strip")), P()),
        check_vma=False,
    )
```

```python
import math

import jax
import jax.numpy as jnp
from jax import lax
from jax.experimental import pallas as pl
from jax.experimental.pallas import tpu as pltpu
from jax.sharding import PartitionSpec as P

HEADS = 8
EPS = 1e-06
TAU = 12.0
BF = jnp.bfloat16
F32 = jnp.float32
LOG2E = math.log2(math.e)
VMEM_LIMIT = 56 * 1024 * 1024


def _dot(a, b):
    return jnp.dot(a, b, preferred_element_type=F32)


def _dot_t(a, b):
    return lax.dot_general(a, b, (((1,), (1,)), ((), ())), preferred_element_type=F32)


def _norm(x, gain):
    return x * lax.rsqrt(jnp.mean(x * x, axis=-1, keepdims=True) + EPS) * gain


def _get(ref, rows):
    return jnp.concatenate([ref[j, rows, :] for j in range(4)], axis=1)


def _put(ref, rows, value):
    for j in range(4):
        ref[j, rows, :] = value[:, 128 * j : 128 * (j + 1)]


def _first_half(shape):
    return lax.broadcasted_iota(jnp.int32, shape, 1) % 128 < 64


def _project(normed, wqkv_ref, seg_ref, rows, q_s, k0_s, k1_s, v0_s, v1_s):
    half = 256
    seg = seg_ref[...]
    even = _first_half((normed.shape[0], half))
    zero = jnp.zeros((normed.shape[0], half), BF)
    one = jnp.ones((normed.shape[0], half), BF)
    for h in range(2):
        lanes = slice(h * half, (h + 1) * half)
        q = _dot(normed, wqkv_ref[:, h * half : (h + 1) * half])
        scale = lax.rsqrt(_dot((q * q).astype(BF), seg) + EPS)
        q_s[rows, lanes] = (q * (scale * (TAU / 64 * LOG2E))).astype(BF)
        k = _dot(normed, wqkv_ref[:, 512 + h * half : 512 + (h + 1) * half])
        scale = lax.rsqrt(_dot((k * k).astype(BF), seg) + EPS)
        k = (k * scale).astype(BF)
        k0_s[rows, lanes] = jnp.where(even, k, zero)
        k1_s[rows, lanes] = jnp.where(even, zero, k)
        v = _dot(normed, wqkv_ref[:, 1024 + h * half : 1024 + (h + 1) * half]).astype(BF)
        v0_s[rows, lanes] = jnp.where(even, v, one)
        v1_s[rows, lanes] = jnp.where(even, one, v)


def _pair(q, k0, k1, v0, v1):
    o0 = _dot(jnp.exp2(_dot_t(q, k0)).astype(BF), v0)
    o1 = _dot(jnp.exp2(_dot_t(q, k1)).astype(BF), v1)
    even = _first_half(o0.shape)
    total = pltpu.roll(jnp.where(even, o1, o0), 64, 1)
    return (jnp.where(even, o0, o1) / total).astype(BF)


def _row_kernel(x_ref, g_ref, wqkv_ref, wo_ref, seg_ref, out_ref, q_s, k0_s, k1_s, v0_s, v1_s, c_s):
    tok, blk = 1024, 256
    gain = g_ref[...]
    for t in range(tok // blk):
        x = x_ref[8 * t : 8 * t + 8, 0].reshape(blk, 512).astype(F32)
        _project(
            _norm(x, gain).astype(BF), wqkv_ref, seg_ref, slice(t * blk, (t + 1) * blk), q_s, k0_s, k1_s, v0_s, v1_s
        )

    def step(i, _):
        lanes = pl.ds(pl.multiple_of(i * 128, 128), 128)
        k0, k1, v0, v1 = k0_s[:, lanes], k1_s[:, lanes], v0_s[:, lanes], v1_s[:, lanes]
        for t in range(tok // blk):
            rows = slice(t * blk, (t + 1) * blk)
            c_s[rows, lanes] = _pair(q_s[rows, lanes], k0, k1, v0, v1)
        return 0

    lax.fori_loop(0, 4, step, 0, unroll=4)
    for t in range(tok // blk):
        x = x_ref[8 * t : 8 * t + 8, 0].reshape(blk, 512).astype(F32)
        y = (x + _dot(c_s[t * blk : (t + 1) * blk, :], wo_ref[...])).astype(BF).reshape(8, 4, 8, 512)
        for b in range(4):
            out_ref[b, 8 * t : 8 * t + 8] = y[:, b]


def row_layer(x, which, gain, wqkv, wo, seg):
    tokens = pltpu.VMEM((1024, 512), BF)
    whole = lambda *shape: pl.BlockSpec(shape, lambda i: (0,) * len(shape))
    return pl.pallas_call(
        _row_kernel,
        grid=(1,),
        out_shape=jax.ShapeDtypeStruct((4, 32, 8, 512), BF),
        in_specs=[
            pl.BlockSpec((32, 1, 32, 512), lambda i: (0, which, 0, 0)),
            whole(1, 512),
            whole(512, 1536),
            whole(512, 512),
            whole(256, 256),
        ],
        out_specs=whole(4, 32, 8, 512),
        scratch_shapes=[tokens] * 6,
        compiler_params=pltpu.CompilerParams(vmem_limit_bytes=VMEM_LIMIT),
        cost_estimate=pl.CostEstimate(flops=12_000_000_000, bytes_accessed=4_000_000, transcendentals=8_000_000),
        name="row_layer",
    )(x, gain, wqkv, wo, seg)


def _rank(named):
    before = lax.broadcasted_iota(jnp.int32, (128, 128), 0) < lax.broadcasted_iota(jnp.int32, (128, 128), 1)
    return _dot(named.astype(F32).astype(BF), before.astype(F32).astype(BF)).astype(jnp.int32)


def _col_kernel(
    x0_ref, x1_ref, g_ref, wqkv_ref, wo_ref, seg_ref, listed_ref, me_ref, y0_ref, y1_ref, y2_ref, y3_ref, send_ref,
    wide_s, q_s, k0_s, k1_s, v0_s, v1_s, c_s,
):
    band, strip = me_ref[0], me_ref[1]
    blk = 256
    gain = g_ref[...]
    for r, x_ref in enumerate((x0_ref, x1_ref)):
        for t in range(4):
            x = x_ref[32 * t : 32 * t + 32].reshape(blk, 512).astype(F32)
            _put(wide_s, slice(r * 1024 + t * blk, r * 1024 + (t + 1) * blk), _norm(x, gain))

    def project(c, _):
        normed = _get(wide_s, pl.ds(c, 256, stride=8)).astype(BF)
        rows = pl.ds(pl.multiple_of(c * 256, 256), 256)
        _project(normed, wqkv_ref, seg_ref, rows, q_s, k0_s, k1_s, v0_s, v1_s)
        return 0

    lax.fori_loop(0, 8, project, 0, unroll=8)

    def attend(c, _):
        rows = pl.ds(pl.multiple_of(c * 256, 256), 256)
        for p in range(4):
            lanes = slice(p * 128, (p + 1) * 128)
            c_s[rows, lanes] = _pair(
                q_s[rows, lanes], k0_s[rows, lanes], k1_s[rows, lanes], v0_s[rows, lanes], v1_s[rows, lanes]
            )
        _put(wide_s, pl.ds(c, 256, stride=8), _dot(c_s[rows, :], wo_ref[...]))
        return 0

    lax.fori_loop(0, 8, attend, 0, unroll=4)
    for d, y_ref in enumerate((y0_ref, y1_ref, y2_ref, y3_ref)):
        to = lax.rem(band + d, 4)
        for r, x_ref in enumerate((x0_ref, x1_ref)):
            x = x_ref[pl.ds(32 * to, 32)].reshape(blk, 512).astype(F32)
            y = x + _get(wide_s, pl.ds(pl.multiple_of(r * 1024 + to * blk, blk), blk))
            y_ref[:, r] = y.astype(BF).reshape(32, 8, 512)
    for d, y_ref in enumerate((y0_ref, y1_ref, y2_ref, y3_ref)):
        lister = lax.rem(band + d, 4) * 32 + strip
        y = y_ref[...].reshape(512, 512)
        cell, owner = listed_ref[lister, 0:1, :], listed_ref[lister, 1:2, :]
        named = lax.broadcasted_iota(jnp.int32, (128, 128), 0) == owner
        rank = _rank(named)
        token = jnp.where((cell % 32) // 8 == band, (cell // 32) * 8 + cell % 8 + 1, 0)
        for m in range(2):
            at = jnp.sum(jnp.where(named & (rank == m), token, 0), axis=1, keepdims=True) - 1
            pick = lax.broadcasted_iota(jnp.int32, (128, 512), 1) == at
            _put(wide_s, pl.ds(2 * d + m, 128, stride=8), _dot(pick.astype(F32).astype(BF), y))
    send_ref[...] = _get(wide_s, slice(0, 1024)).astype(BF).reshape(128, 8, 512)


VM = pl.BlockSpec(memory_space=pltpu.VMEM)
SM = pl.BlockSpec(memory_space=pltpu.SMEM)
ANY = pl.BlockSpec(memory_space=pl.ANY)


def col_layer(x0, x1, gain, wqkv, wo, seg, listed, me):
    tokens = pltpu.VMEM((2048, 512), BF)
    part = jax.ShapeDtypeStruct((32, 2, 8, 512), BF)
    return pl.pallas_call(
        _col_kernel,
        out_shape=(part,) * 4 + (jax.ShapeDtypeStruct((128, 8, 512), BF),),
        in_specs=[VM] * 7 + [SM],
        out_specs=(VM,) * 5,
        scratch_shapes=[pltpu.VMEM((4, 2048, 128), F32)] + [tokens] * 6,
        compiler_params=pltpu.CompilerParams(vmem_limit_bytes=VMEM_LIMIT),
        cost_estimate=pl.CostEstimate(flops=12_000_000_000, bytes_accessed=9_000_000, transcendentals=4_000_000),
        name="col_layer",
    )(x0, x1, gain, wqkv, wo, seg, listed, me)


def _decode_kernel(f_ref, w1_ref, w2_ref, listed_ref, me_ref, out_ref, logit_s):
    w2 = jnp.broadcast_to(w2_ref[...], (128, 512))
    for t in range(4):
        feats = f_ref[32 * t : 32 * t + 32].reshape(256, 512)
        hidden = jax.nn.gelu(_dot(feats, w1_ref[...])).astype(BF)
        logit_s[t * 256 : (t + 1) * 256, :] = _dot_t(hidden, w2)
    cell, owner, cap = listed_ref[:, 0, :], listed_ref[:, 1, :], listed_ref[:, 2, :]
    named = owner == me_ref[0] * 32 + me_ref[1]
    rank = _rank(named)
    home = (cell % 32) // 8 + 1
    lane = lax.broadcasted_iota(jnp.int32, (32, 128), 1)
    values = []
    for k in range(8):
        logit = logit_s[pl.ds(k, 128, stride=8), :]
        values.append(jnp.maximum(logit, 0.0) + jnp.log1p(jnp.exp(-jnp.abs(logit))))
    total = jnp.zeros((1, 128), F32)
    found = []
    for m in range(2):
        one = named & (rank == m)
        homes = jnp.sum(jnp.where(one, home, 0), axis=1, keepdims=True) - 1
        caps = jnp.sum(jnp.where(one, cap, 0), axis=1, keepdims=True).astype(F32) * 0.001
        for b in range(4):
            value = jnp.zeros((32, 128), F32)
            for d in range(4):
                h = (b - d) % 4
                value = jnp.where(
                    homes[32 * b : 32 * b + 32] == h, values[2 * d + m][32 * h : 32 * h + 32], value
                )
            found.append(value)
            total = total + jnp.sum(value * caps[32 * b : 32 * b + 32], axis=0, keepdims=True)
    for b in range(4):
        rows = jnp.where(lane == 0, found[b], jnp.where(lane == 1, found[4 + b], total))
        out_ref[32 * b : 32 * b + 32, :] = rows


def decode(features, w1, w2, listed, me):
    return pl.pallas_call(
        _decode_kernel,
        out_shape=jax.ShapeDtypeStruct((128, 128), F32),
        in_specs=[VM] * 4 + [SM],
        out_specs=VM,
        scratch_shapes=[pltpu.VMEM((1024, 128), F32)],
        compiler_params=pltpu.CompilerParams(vmem_limit_bytes=VMEM_LIMIT),
        cost_estimate=pl.CostEstimate(flops=600_000_000, bytes_accessed=2_000_000, transcendentals=600_000),
        name="decode",
    )(features, w1, w2, listed, me)


def _power_kernel(back_ref, listed_ref, me_ref, power_ref, fleet_ref):
    back = back_ref[...]
    mine = me_ref[0] * 32 + me_ref[1]
    named = lax.broadcasted_iota(jnp.int32, (128, 128), 0) == listed_ref[mine, 1:2, :]
    rank = _rank(named)
    value = jnp.where(named, jnp.where(rank == 0, back[:, 0:1], back[:, 1:2]), 0.0)
    kilowatts = listed_ref[mine, 2:3, :].astype(F32)
    power_ref[...] = kilowatts * 0.001 * jnp.sum(value, axis=0, keepdims=True)
    fleet_ref[...] = jnp.sum(back[:, 2:3], axis=0, keepdims=True) / 16384.0


def power(back, listed, me):
    return pl.pallas_call(
        _power_kernel,
        out_shape=(jax.ShapeDtypeStruct((1, 128), F32), jax.ShapeDtypeStruct((1, 1), F32)),
        in_specs=[VM, VM, SM],
        out_specs=(VM, VM),
        name="plant_power",
    )(back, listed, me)


def _assemble_kernel(p0_ref, p1_ref, p2_ref, p3_ref, me_ref, out_ref, sems):
    copies = []
    for d, p_ref in enumerate((p0_ref, p1_ref, p2_ref, p3_ref)):
        place = lax.rem(me_ref[0] + 4 - d, 4)
        copies.append(pltpu.make_async_copy(p_ref, out_ref.at[:, place], sems.at[d]))
    for copy in copies:
        copy.start()
    for copy in copies:
        copy.wait()


def assemble(parts, me):
    return pl.pallas_call(
        _assemble_kernel,
        out_shape=jax.ShapeDtypeStruct((64, 4, 8, 512), BF),
        in_specs=[ANY] * 4 + [SM],
        out_specs=ANY,
        scratch_shapes=[pltpu.SemaphoreType.DMA((4,))],
        name="assemble",
    )(*parts, me)


def body(
    cloud_field, row_gain, row_qkv, row_out, col_gain, col_qkv, col_out,
    plant_cell, plant_decoder_device, plant_capacity, decode_first, decode_second,
):
    everyone = ("band", "strip")
    a2a = lambda x, axis: lax.all_to_all(x, axis, split_axis=0, concat_axis=0, tiled=True)
    seg_of = jnp.arange(256) // 64
    seg = jnp.where(seg_of[:, None] == seg_of[None, :], 1.0 / 64, 0.0).astype(BF)
    tokens = a2a(cloud_field.reshape(32, 2, 32, 512), "strip")

    me = jnp.stack([lax.axis_index("band"), lax.axis_index("strip")]).astype(jnp.int32)
    listed = jnp.stack([plant_cell, plant_decoder_device[:, 0], plant_capacity])
    listed = lax.all_gather(jnp.pad(listed, ((0, 13), (0, 0))), everyone)

    row_args = (row_gain.reshape(1, 512), row_qkv, row_out, seg)
    sent0 = a2a(row_layer(tokens, 0, *row_args).reshape(128, 8, 512), everyone)
    sent1 = a2a(row_layer(tokens, 1, *row_args).reshape(128, 8, 512), everyone)
    *columns, features = col_layer(sent0, sent1, col_gain.reshape(1, 512), col_qkv, col_out, seg, listed, me)
    features = a2a(features, everyone)
    columns = [c.reshape(64, 8, 512) for c in columns]
    parts = columns[:1] + [
        lax.ppermute(columns[d], "band", [(i, (i + d) % 4) for i in range(4)]) for d in (1, 2, 3)
    ]
    final_field = assemble(parts, me).reshape(64, 32, 512)
    payload = decode(features, decode_first, decode_second, listed, me)
    back = a2a(payload.reshape(128, 1, 128), everyone).reshape(128, 128)
    plant_power, fleet = power(back, listed, me)
    return (final_field, plant_power.reshape(128), fleet.reshape(()))


def solution(mesh):
    return jax.shard_map(
        body,
        mesh=mesh,
        in_specs=(
            P("band", "strip", None),
            P(),
            P(),
            P(),
            P(),
            P(),
            P(),
            P(("band", "strip")),
            P(("band", "strip"), None),
            P(("band", "strip")),
            P(("band", "strip"), None),
            P(("band", "strip"), None),
        ),
        out_specs=(P("band", "strip", None), P(("band", "strip")), P()),
        check_vma=False,
    )
```

```python
import functools
import math

import jax
import jax.numpy as jnp
from jax import lax
from jax.experimental import pallas as pl
from jax.experimental.pallas import tpu as pltpu
from jax.sharding import PartitionSpec as P

HEADS = 8
EPS = 1e-06
TAU = 12.0
BF = jnp.bfloat16
F32 = jnp.float32
LOG2E = math.log2(math.e)
VMEM_ROW = 24 * 1024 * 1024
VMEM_COL = 36 * 1024 * 1024
VMEM_SMALL = 8 * 1024 * 1024


def _dot(a, b):
    return jnp.dot(a, b, preferred_element_type=F32)


def _dot_t(a, b):
    return lax.dot_general(a, b, (((1,), (1,)), ((), ())), preferred_element_type=F32)


def _norm(x, gain):
    return x * lax.rsqrt(jnp.mean(x * x, axis=-1, keepdims=True) + EPS) * gain


def _first_half(shape):
    return lax.broadcasted_iota(jnp.int32, shape, 1) % 128 < 64


def _segments():
    a, b = (lax.broadcasted_iota(jnp.int32, (256, 256), i) // 64 for i in (0, 1))
    return jnp.where(a == b, 1.0 / 64, 0.0).astype(BF)


def _turn(back):
    a, b = (lax.broadcasted_iota(jnp.int32, (256, 256), 1 - i if back else i) for i in (0, 1))
    return jnp.where(a == b % 8 * 32 + b // 8, 1.0, 0.0).astype(BF)


def _project(normed, wqkv_ref, seg, rows, q_s, k0_s, k1_s, v0_s, v1_s):
    half = 256
    even = _first_half((normed.shape[0], half))
    zero = jnp.zeros((normed.shape[0], half), BF)
    one = jnp.ones((normed.shape[0], half), BF)
    for h in range(2):
        lanes = slice(h * half, (h + 1) * half)
        q = _dot(normed, wqkv_ref[:, h * half : (h + 1) * half])
        scale = lax.rsqrt(_dot((q * q).astype(BF), seg) + EPS)
        q_s[rows, lanes] = (q * (scale * (TAU / 64 * LOG2E))).astype(BF)
        k = _dot(normed, wqkv_ref[:, 512 + h * half : 512 + (h + 1) * half])
        scale = lax.rsqrt(_dot((k * k).astype(BF), seg) + EPS)
        k = (k * scale).astype(BF)
        k0_s[rows, lanes] = jnp.where(even, k, zero)
        k1_s[rows, lanes] = jnp.where(even, zero, k)
        v = _dot(normed, wqkv_ref[:, 1024 + h * half : 1024 + (h + 1) * half]).astype(BF)
        v0_s[rows, lanes] = jnp.where(even, v, one)
        v1_s[rows, lanes] = jnp.where(even, one, v)


def _pair(q, k0, k1, v0, v1):
    o0 = _dot(jnp.exp2(_dot_t(q, k0)).astype(BF), v0)
    o1 = _dot(jnp.exp2(_dot_t(q, k1)).astype(BF), v1)
    even = _first_half(o0.shape)
    total = pltpu.roll(jnp.where(even, o1, o0), 64, 1)
    return (jnp.where(even, o0, o1) / total).astype(BF)


def _row_kernel(
    which, x_ref, g_ref, wqkv_any, wo_any, out_any, wqkv_s, wo_s, out_s, q_s, k0_s, k1_s, v0_s, v1_s, c_s, sems
):
    wqkv_copy = pltpu.make_async_copy(wqkv_any, wqkv_s, sems.at[0])
    wo_copy = pltpu.make_async_copy(wo_any, wo_s, sems.at[1])
    wqkv_copy.start()
    wo_copy.start()
    tok, blk = 1024, 256
    gain = g_ref[...]
    seg = _segments()
    wqkv_copy.wait()
    for t in range(tok // blk):
        x = x_ref[8 * t : 8 * t + 8, which].reshape(blk, 512).astype(F32)
        _project(
            _norm(x, gain).astype(BF), wqkv_s, seg, slice(t * blk, (t + 1) * blk), q_s, k0_s, k1_s, v0_s, v1_s
        )
    for p in range(4):
        lanes = slice(p * 128, (p + 1) * 128)
        k0, k1, v0, v1 = k0_s[:, lanes], k1_s[:, lanes], v0_s[:, lanes], v1_s[:, lanes]
        for t in range(tok // blk):
            rows = slice(t * blk, (t + 1) * blk)
            c_s[rows, lanes] = _pair(q_s[rows, lanes], k0, k1, v0, v1)
    wo_copy.wait()
    sent = []
    for t in range(tok // blk):
        x = x_ref[8 * t : 8 * t + 8, which].reshape(blk, 512).astype(F32)
        y = (x + _dot(c_s[t * blk : (t + 1) * blk, :], wo_s[...])).astype(BF).reshape(8, 4, 8, 512)
        for b in range(4):
            out_s[b, 8 * t : 8 * t + 8] = y[:, b]
        part = slice(8 * t, 8 * t + 8)
        sent.append(pltpu.make_async_copy(out_s.at[:, part], out_any.at[:, part], sems.at[2 + t]))
        sent[-1].start()
    for copy in sent:
        copy.wait()


def _rank(named):
    before = lax.broadcasted_iota(jnp.int32, (128, 128), 0) < lax.broadcasted_iota(jnp.int32, (128, 128), 1)
    return _dot(named.astype(F32).astype(BF), before.astype(F32).astype(BF)).astype(jnp.int32)


def _col_kernel(
    x0_ref, x1_ref, g_ref, wqkv_any, wo_any, listed_ref, me_ref, y0_any, y1_any, y2_any, y3_any, send_any,
    wqkv_s, wo_s, y_s, send_s, q_s, k0_s, k1_s, v0_s, v1_s, c_s, t_s, sems,
):
    wqkv_copy = pltpu.make_async_copy(wqkv_any, wqkv_s, sems.at[0])
    wo_copy = pltpu.make_async_copy(wo_any, wo_s, sems.at[1])
    wqkv_copy.start()
    wo_copy.start()
    band, strip = me_ref[0], me_ref[1]
    blk = 256
    gain = g_ref[...]
    seg, apart, together = _segments(), _turn(False), _turn(True)
    for r, x_ref in enumerate((x0_ref, x1_ref)):
        for t in range(4):
            x = x_ref[32 * t : 32 * t + 32].reshape(blk, 512).astype(F32)
            normed = _dot(apart, _norm(x, gain).astype(BF)).astype(BF)
            for c in range(8):
                at = c * 256 + r * 128 + t * 32
                t_s[at : at + 32, :] = normed[32 * c : 32 * c + 32]
    wqkv_copy.wait()
    for c in range(8):
        rows = slice(c * blk, (c + 1) * blk)
        _project(t_s[rows, :], wqkv_s, seg, rows, q_s, k0_s, k1_s, v0_s, v1_s)
    for c in range(8):
        rows = slice(c * blk, (c + 1) * blk)
        for p in range(4):
            lanes = slice(p * 128, (p + 1) * 128)
            c_s[rows, lanes] = _pair(
                q_s[rows, lanes], k0_s[rows, lanes], k1_s[rows, lanes], v0_s[rows, lanes], v1_s[rows, lanes]
            )
    wo_copy.wait()
    sent = []
    for d, y_any in enumerate((y0_any, y1_any, y2_any, y3_any)):
        to = lax.rem(band + d, 4)
        for r, x_ref in enumerate((x0_ref, x1_ref)):
            context = [c_s[pl.ds(pl.multiple_of(c * 256 + r * 128 + to * 32, 32), 32), :] for c in range(8)]
            context = _dot(together, jnp.concatenate(context, axis=0)).astype(BF)
            x = x_ref[pl.ds(32 * to, 32)].reshape(blk, 512).astype(F32)
            y_s[d, :, r] = (x + _dot(context, wo_s[...])).astype(BF).reshape(32, 8, 512)
        sent.append(pltpu.make_async_copy(y_s.at[d], y_any, sems.at[2 + d]))
        sent[-1].start()
    for d in range(4):
        lister = lax.rem(band + d, 4) * 32 + strip
        y = y_s[d].reshape(512, 512)
        cell, owner = listed_ref[0, pl.ds(lister, 1), :], listed_ref[1, pl.ds(lister, 1), :]
        named = lax.broadcasted_iota(jnp.int32, (128, 128), 0) == owner
        rank = _rank(named)
        token = jnp.where((cell % 32) // 8 == band, (cell // 32) * 8 + cell % 8 + 1, 0)
        for m in range(2):
            at = jnp.sum(jnp.where(named & (rank == m), token, 0), axis=1, keepdims=True) - 1
            pick = lax.broadcasted_iota(jnp.int32, (128, 512), 1) == at
            k = 2 * d + m
            t_s[128 * k : 128 * (k + 1), :] = _dot(pick.astype(F32).astype(BF), y).astype(BF)
    for g in range(4):
        features = [t_s[128 * k + 32 * g : 128 * k + 32 * g + 32, :] for k in range(8)]
        features = _dot(together, jnp.concatenate(features, axis=0))
        part = slice(32 * g, 32 * g + 32)
        send_s[part] = features.astype(BF).reshape(32, 8, 512)
        sent.append(pltpu.make_async_copy(send_s.at[part], send_any.at[part], sems.at[6 + g]))
        sent[-1].start()
    for copy in sent:
        copy.wait()


def _near(*arrays):
    return [pltpu.with_memory_space_constraint(a, pltpu.VMEM) for a in arrays]


def _far(*arrays):
    return [pltpu.with_memory_space_constraint(a, pltpu.HBM) for a in arrays]


VM = pl.BlockSpec(memory_space=pltpu.VMEM)
SM = pl.BlockSpec(memory_space=pltpu.SMEM)
ANY = pl.BlockSpec(memory_space=pl.ANY)


def row_layer(x, which, gain, wqkv, wo):
    tokens = pltpu.VMEM((1024, 512), BF)
    return pl.pallas_call(
        functools.partial(_row_kernel, which),
        out_shape=pltpu.HBM((4, 32, 8, 512), BF),
        in_specs=[VM] * 2 + [ANY] * 2,
        out_specs=ANY,
        scratch_shapes=[pltpu.VMEM((512, 1536), BF), pltpu.VMEM((512, 512), BF), pltpu.VMEM((4, 32, 8, 512), BF)]
        + [tokens] * 6
        + [pltpu.SemaphoreType.DMA((6,))],
        compiler_params=pltpu.CompilerParams(vmem_limit_bytes=VMEM_ROW),
        cost_estimate=pl.CostEstimate(flops=12_000_000_000, bytes_accessed=4_000_000, transcendentals=8_000_000),
        name="row_layer",
    )(*_near(x), gain, *_far(wqkv, wo))


def col_layer(x0, x1, gain, wqkv, wo, listed, me):
    tokens = pltpu.VMEM((2048, 512), BF)
    return pl.pallas_call(
        _col_kernel,
        out_shape=(pltpu.HBM((32, 2, 8, 512), BF),) * 4 + (pltpu.HBM((128, 8, 512), BF),),
        in_specs=[VM] * 3 + [ANY] * 2 + [VM, SM],
        out_specs=(ANY,) * 5,
        scratch_shapes=[
            pltpu.VMEM((512, 1536), BF),
            pltpu.VMEM((512, 512), BF),
            pltpu.VMEM((4, 32, 2, 8, 512), BF),
            pltpu.VMEM((128, 8, 512), BF),
        ]
        + [tokens] * 7
        + [pltpu.SemaphoreType.DMA((10,))],
        compiler_params=pltpu.CompilerParams(vmem_limit_bytes=VMEM_COL),
        cost_estimate=pl.CostEstimate(flops=12_000_000_000, bytes_accessed=9_000_000, transcendentals=4_000_000),
        name="col_layer",
    )(*_near(x0, x1), gain, *_far(wqkv, wo), *_near(listed), me)


def _decode_kernel(f_ref, w1_ref, w2_ref, listed_ref, me_ref, out_ref, logit_s):
    w2 = jnp.broadcast_to(w2_ref[...], (128, 512))
    for t in range(4):
        feats = f_ref[32 * t : 32 * t + 32].reshape(256, 512)
        hidden = jax.nn.gelu(_dot(feats, w1_ref[...])).astype(BF)
        logit_s[t * 256 : (t + 1) * 256, :] = _dot_t(hidden, w2)
    cell, owner, cap = listed_ref[0], listed_ref[1], listed_ref[2]
    named = owner == me_ref[0] * 32 + me_ref[1]
    rank = _rank(named)
    home = (cell % 32) // 8 + 1
    lane = lax.broadcasted_iota(jnp.int32, (32, 128), 1)
    values = []
    for k in range(8):
        logit = logit_s[pl.ds(k, 128, stride=8), :]
        values.append(jnp.maximum(logit, 0.0) + jnp.log1p(jnp.exp(-jnp.abs(logit))))
    total = jnp.zeros((1, 128), F32)
    found = []
    for m in range(2):
        one = named & (rank == m)
        homes = jnp.sum(jnp.where(one, home, 0), axis=1, keepdims=True) - 1
        caps = jnp.sum(jnp.where(one, cap, 0), axis=1, keepdims=True).astype(F32) * 0.001
        for b in range(4):
            value = jnp.zeros((32, 128), F32)
            for d in range(4):
                h = (b - d) % 4
                value = jnp.where(
                    homes[32 * b : 32 * b + 32] == h, values[2 * d + m][32 * h : 32 * h + 32], value
                )
            found.append(value)
            total = total + jnp.sum(value * caps[32 * b : 32 * b + 32], axis=0, keepdims=True)
    for b in range(4):
        rows = jnp.where(lane == 0, found[b], jnp.where(lane == 1, found[4 + b], total))
        out_ref[32 * b : 32 * b + 32, :] = rows


def decode(features, w1, w2, listed, me):
    return pl.pallas_call(
        _decode_kernel,
        out_shape=jax.ShapeDtypeStruct((128, 128), F32),
        in_specs=[VM] * 4 + [SM],
        out_specs=VM,
        scratch_shapes=[pltpu.VMEM((1024, 128), F32)],
        compiler_params=pltpu.CompilerParams(vmem_limit_bytes=VMEM_SMALL),
        cost_estimate=pl.CostEstimate(flops=600_000_000, bytes_accessed=2_000_000, transcendentals=600_000),
        name="decode",
    )(*_near(features, w1), w2, *_near(listed), me)


def _power_kernel(back_ref, listed_ref, me_ref, power_ref, fleet_ref):
    back = back_ref[...]
    mine = me_ref[0] * 32 + me_ref[1]
    named = lax.broadcasted_iota(jnp.int32, (128, 128), 0) == listed_ref[1, pl.ds(mine, 1), :]
    rank = _rank(named)
    value = jnp.where(named, jnp.where(rank == 0, back[:, 0:1], back[:, 1:2]), 0.0)
    kilowatts = listed_ref[2, pl.ds(mine, 1), :].astype(F32)
    power_ref[...] = kilowatts * 0.001 * jnp.sum(value, axis=0, keepdims=True)
    fleet_ref[...] = jnp.sum(back[:, 2:3], axis=0, keepdims=True) / 16384.0


def power(back, listed, me):
    return pl.pallas_call(
        _power_kernel,
        out_shape=(jax.ShapeDtypeStruct((1, 128), F32), jax.ShapeDtypeStruct((1, 1), F32)),
        in_specs=[VM, VM, SM],
        out_specs=(VM, VM),
        name="plant_power",
    )(*_near(back, listed), me)


def _assemble_kernel(p0_ref, p1_ref, p2_ref, p3_ref, me_ref, out_any, sems):
    copies = []
    for d, p_ref in enumerate((p0_ref, p1_ref, p2_ref, p3_ref)):
        place = lax.rem(me_ref[0] + 4 - d, 4)
        copies.append(pltpu.make_async_copy(p_ref, out_any.at[:, place], sems.at[d]))
        copies[-1].start()
    for copy in copies:
        copy.wait()


def assemble(parts, me):
    return pl.pallas_call(
        _assemble_kernel,
        out_shape=pltpu.HBM((64, 4, 8, 512), BF),
        in_specs=[VM] * 4 + [SM],
        out_specs=ANY,
        scratch_shapes=[pltpu.SemaphoreType.DMA((4,))],
        compiler_params=pltpu.CompilerParams(vmem_limit_bytes=VMEM_SMALL),
        cost_estimate=pl.CostEstimate(flops=0, bytes_accessed=4_000_000, transcendentals=0),
        name="assemble",
    )(*_near(*parts), me)


def body(
    cloud_field, row_gain, row_qkv, row_out, col_gain, col_qkv, col_out,
    plant_cell, plant_decoder_device, plant_capacity, decode_first, decode_second,
):
    everyone = ("band", "strip")
    a2a = lambda x, axis: lax.all_to_all(x, axis, split_axis=0, concat_axis=0, tiled=True)
    tokens = a2a(cloud_field.reshape(32, 2, 32, 512), "strip")

    me = jnp.stack([lax.axis_index("band"), lax.axis_index("strip")]).astype(jnp.int32)
    listed = jnp.stack([plant_cell, plant_decoder_device[:, 0], plant_capacity])
    listed = lax.all_gather(jnp.pad(listed, ((0, 13), (0, 0))), everyone)[:, :3].transpose(1, 0, 2)

    row_args = (row_gain.reshape(1, 512), row_qkv, row_out)
    sent0 = a2a(row_layer(tokens, 0, *row_args).reshape(128, 8, 512), everyone)
    sent1 = a2a(row_layer(tokens, 1, *row_args).reshape(128, 8, 512), everyone)
    *columns, features = col_layer(sent0, sent1, col_gain.reshape(1, 512), col_qkv, col_out, listed, me)
    features = a2a(features, everyone)
    columns = [c.reshape(64, 8, 512) for c in columns]
    parts = columns[:1] + [
        lax.ppermute(columns[d], "band", [(i, (i + d) % 4) for i in range(4)]) for d in (1, 2, 3)
    ]
    final_field = assemble(parts, me).reshape(64, 32, 512)
    payload = decode(features, decode_first, decode_second, listed, me)
    back = a2a(payload.reshape(128, 1, 128), everyone).reshape(128, 128)
    plant_power, fleet = power(back, listed, me)
    return (final_field, plant_power.reshape(128), fleet.reshape(()))


def solution(mesh):
    return jax.shard_map(
        body,
        mesh=mesh,
        in_specs=(
            P("band", "strip", None),
            P(),
            P(),
            P(),
            P(),
            P(),
            P(),
            P(("band", "strip")),
            P(("band", "strip"), None),
            P(("band", "strip")),
            P(("band", "strip"), None),
            P(("band", "strip"), None),
        ),
        out_specs=(P("band", "strip", None), P(("band", "strip")), P()),
        check_vma=False,
    )
```

```python
import functools
import math

import jax
import jax.numpy as jnp
from jax import lax
from jax.experimental import pallas as pl
from jax.experimental.pallas import tpu as pltpu
from jax.sharding import PartitionSpec as P

HEADS = 8
EPS = 1e-06
TAU = 12.0
BF = jnp.bfloat16
F32 = jnp.float32
LOG2E = math.log2(math.e)
VMEM_ROW = 24 * 1024 * 1024
VMEM_COL = 36 * 1024 * 1024
VMEM_SMALL = 8 * 1024 * 1024


def _dot(a, b):
    return jnp.dot(a, b, preferred_element_type=F32)


def _dot_t(a, b):
    return lax.dot_general(a, b, (((1,), (1,)), ((), ())), preferred_element_type=F32)


def _norm(x, gain):
    return x * lax.rsqrt(jnp.mean(x * x, axis=-1, keepdims=True) + EPS) * gain


def _first_half(shape):
    return lax.broadcasted_iota(jnp.int32, shape, 1) % 128 < 64


def _segments():
    a, b = (lax.broadcasted_iota(jnp.int32, (256, 256), i) // 64 for i in (0, 1))
    return jnp.where(a == b, 1.0 / 64, 0.0).astype(BF)


def _turn(back):
    a, b = (lax.broadcasted_iota(jnp.int32, (256, 256), 1 - i if back else i) for i in (0, 1))
    return jnp.where(a == b % 8 * 32 + b // 8, 1.0, 0.0).astype(BF)


def _project(normed, wqkv_ref, seg, rows, q_s, k0_s, k1_s, v0_s, v1_s):
    half = 256
    even = _first_half((normed.shape[0], half))
    zero = jnp.zeros((normed.shape[0], half), BF)
    one = jnp.ones((normed.shape[0], half), BF)
    for h in range(2):
        lanes = slice(h * half, (h + 1) * half)
        q = _dot(normed, wqkv_ref[:, h * half : (h + 1) * half])
        scale = lax.rsqrt(_dot((q * q).astype(BF), seg) + EPS)
        q_s[rows, lanes] = (q * (scale * (TAU / 64 * LOG2E))).astype(BF)
        k = _dot(normed, wqkv_ref[:, 512 + h * half : 512 + (h + 1) * half])
        scale = lax.rsqrt(_dot((k * k).astype(BF), seg) + EPS)
        k = (k * scale).astype(BF)
        k0_s[rows, lanes] = jnp.where(even, k, zero)
        k1_s[rows, lanes] = jnp.where(even, zero, k)
        v = _dot(normed, wqkv_ref[:, 1024 + h * half : 1024 + (h + 1) * half]).astype(BF)
        v0_s[rows, lanes] = jnp.where(even, v, one)
        v1_s[rows, lanes] = jnp.where(even, one, v)


def _pair(q, k0, k1, v0, v1):
    o0 = _dot(jnp.exp2(_dot_t(q, k0)).astype(BF), v0)
    o1 = _dot(jnp.exp2(_dot_t(q, k1)).astype(BF), v1)
    even = _first_half(o0.shape)
    total = pltpu.roll(jnp.where(even, o1, o0), 64, 1)
    return (jnp.where(even, o0, o1) / total).astype(BF)


def _row_kernel(
    which, x_ref, g_ref, wqkv_any, wo_any, out_any, wqkv_s, wo_s, out_s, q_s, k0_s, k1_s, v0_s, v1_s, c_s, sems
):
    wqkv_copy = pltpu.make_async_copy(wqkv_any, wqkv_s, sems.at[0])
    wo_copy = pltpu.make_async_copy(wo_any, wo_s, sems.at[1])
    wqkv_copy.start()
    wo_copy.start()
    tok, blk = 1024, 256
    gain = g_ref[...]
    seg = _segments()
    wqkv_copy.wait()
    for t in range(tok // blk):
        x = x_ref[8 * t : 8 * t + 8, which].reshape(blk, 512).astype(F32)
        _project(
            _norm(x, gain).astype(BF), wqkv_s, seg, slice(t * blk, (t + 1) * blk), q_s, k0_s, k1_s, v0_s, v1_s
        )
    for p in range(4):
        lanes = slice(p * 128, (p + 1) * 128)
        k0, k1, v0, v1 = k0_s[:, lanes], k1_s[:, lanes], v0_s[:, lanes], v1_s[:, lanes]
        for t in range(tok // blk):
            rows = slice(t * blk, (t + 1) * blk)
            c_s[rows, lanes] = _pair(q_s[rows, lanes], k0, k1, v0, v1)
    wo_copy.wait()
    sent = []
    for t in range(tok // blk):
        x = x_ref[8 * t : 8 * t + 8, which].reshape(blk, 512).astype(F32)
        y = (x + _dot(c_s[t * blk : (t + 1) * blk, :], wo_s[...])).astype(BF).reshape(8, 4, 8, 512)
        for b in range(4):
            out_s[b, 8 * t : 8 * t + 8] = y[:, b]
        part = slice(8 * t, 8 * t + 8)
        sent.append(pltpu.make_async_copy(out_s.at[:, part], out_any.at[:, part], sems.at[2 + t]))
        sent[-1].start()
    for copy in sent:
        copy.wait()


def _rank(named):
    before = lax.broadcasted_iota(jnp.int32, (128, 128), 0) < lax.broadcasted_iota(jnp.int32, (128, 128), 1)
    return _dot(named.astype(F32).astype(BF), before.astype(F32).astype(BF)).astype(jnp.int32)


def _col_kernel(
    x0_ref, x1_ref, g_ref, wqkv_any, wo_any, listed_ref, me_ref, y0_any, y1_any, y2_any, y3_any, send_any,
    wqkv_s, wo_s, y_s, send_s, q_s, k0_s, k1_s, v0_s, v1_s, c_s, t_s, sems,
):
    wqkv_copy = pltpu.make_async_copy(wqkv_any, wqkv_s, sems.at[0])
    wo_copy = pltpu.make_async_copy(wo_any, wo_s, sems.at[1])
    wqkv_copy.start()
    wo_copy.start()
    band = me_ref[0]
    blk = 256
    gain = g_ref[...]
    seg, apart, together = _segments(), _turn(False), _turn(True)
    for r, x_ref in enumerate((x0_ref, x1_ref)):
        for t in range(4):
            x = x_ref[32 * t : 32 * t + 32].reshape(blk, 512).astype(F32)
            normed = _dot(apart, _norm(x, gain).astype(BF)).astype(BF)
            for c in range(8):
                at = c * 256 + r * 128 + t * 32
                t_s[at : at + 32, :] = normed[32 * c : 32 * c + 32]
    wqkv_copy.wait()
    for c in range(8):
        rows = slice(c * blk, (c + 1) * blk)
        _project(t_s[rows, :], wqkv_s, seg, rows, q_s, k0_s, k1_s, v0_s, v1_s)
    for c in range(8):
        rows = slice(c * blk, (c + 1) * blk)
        for p in range(4):
            lanes = slice(p * 128, (p + 1) * 128)
            c_s[rows, lanes] = _pair(
                q_s[rows, lanes], k0_s[rows, lanes], k1_s[rows, lanes], v0_s[rows, lanes], v1_s[rows, lanes]
            )
    wo_copy.wait()
    sent = []
    for d, y_any in enumerate((y0_any, y1_any, y2_any, y3_any)):
        to = lax.rem(band + d, 4)
        for r, x_ref in enumerate((x0_ref, x1_ref)):
            context = [c_s[pl.ds(pl.multiple_of(c * 256 + r * 128 + to * 32, 32), 32), :] for c in range(8)]
            context = _dot(together, jnp.concatenate(context, axis=0)).astype(BF)
            x = x_ref[pl.ds(32 * to, 32)].reshape(blk, 512).astype(F32)
            y_s[d, :, r] = (x + _dot(context, wo_s[...])).astype(BF).reshape(32, 8, 512)
        sent.append(pltpu.make_async_copy(y_s.at[d], y_any, sems.at[2 + d]))
        sent[-1].start()
    lane = lax.broadcasted_iota(jnp.int32, (128, 128), 1)
    for d in range(4):
        lister = lax.rem(band + d, 4)
        y = y_s[d].reshape(512, 512)
        cell, owner, cap = (listed_ref[i, pl.ds(lister, 1), :] for i in range(3))
        named = lax.broadcasted_iota(jnp.int32, (128, 128), 0) == owner
        rank = _rank(named)
        home = (cell % 32) // 8
        token = jnp.where(home == band, (cell // 32) * 8 + cell % 8 + 1, 0)
        for m in range(2):
            of = lambda v: jnp.sum(jnp.where(named & (rank == m), v, 0), axis=1, keepdims=True)
            at = of(token) - 1
            pick = lax.broadcasted_iota(jnp.int32, (128, 512), 1) == at
            k = 2 * d + m
            feature = _dot(pick.astype(F32).astype(BF), y)
            t_s[128 * k : 128 * (k + 1), 128:] = feature[:, 128:].astype(BF)
            note = jnp.where(lane == 0, of(home + 1), jnp.where(lane == 1, of(cap // 128), of(cap % 128)))
            note = jnp.where(lane < 3, note, 0).astype(F32)
            t_s[128 * k : 128 * (k + 1), :128] = jnp.where(at < 0, note, feature[:, :128]).astype(BF)
    for g in range(4):
        features = [t_s[128 * k + 32 * g : 128 * k + 32 * g + 32, :] for k in range(8)]
        features = _dot(together, jnp.concatenate(features, axis=0))
        part = slice(32 * g, 32 * g + 32)
        send_s[part] = features.astype(BF).reshape(32, 8, 512)
        sent.append(pltpu.make_async_copy(send_s.at[part], send_any.at[part], sems.at[6 + g]))
        sent[-1].start()
    for copy in sent:
        copy.wait()


def _near(*arrays):
    return [pltpu.with_memory_space_constraint(a, pltpu.VMEM) for a in arrays]


def _far(*arrays):
    return [pltpu.with_memory_space_constraint(a, pltpu.HBM) for a in arrays]


VM = pl.BlockSpec(memory_space=pltpu.VMEM)
SM = pl.BlockSpec(memory_space=pltpu.SMEM)
ANY = pl.BlockSpec(memory_space=pl.ANY)


def row_layer(x, which, gain, wqkv, wo):
    tokens = pltpu.VMEM((1024, 512), BF)
    return pl.pallas_call(
        functools.partial(_row_kernel, which),
        out_shape=pltpu.HBM((4, 32, 8, 512), BF),
        in_specs=[VM] * 2 + [ANY] * 2,
        out_specs=ANY,
        scratch_shapes=[pltpu.VMEM((512, 1536), BF), pltpu.VMEM((512, 512), BF), pltpu.VMEM((4, 32, 8, 512), BF)]
        + [tokens] * 6
        + [pltpu.SemaphoreType.DMA((6,))],
        compiler_params=pltpu.CompilerParams(vmem_limit_bytes=VMEM_ROW),
        cost_estimate=pl.CostEstimate(flops=12_000_000_000, bytes_accessed=4_000_000, transcendentals=8_000_000),
        name="row_layer",
    )(*_near(x), gain, *_far(wqkv, wo))


def col_layer(x0, x1, gain, wqkv, wo, listed, me):
    tokens = pltpu.VMEM((2048, 512), BF)
    return pl.pallas_call(
        _col_kernel,
        out_shape=(pltpu.HBM((32, 2, 8, 512), BF),) * 4 + (pltpu.HBM((128, 8, 512), BF),),
        in_specs=[VM] * 3 + [ANY] * 2 + [VM, SM],
        out_specs=(ANY,) * 5,
        scratch_shapes=[
            pltpu.VMEM((512, 1536), BF),
            pltpu.VMEM((512, 512), BF),
            pltpu.VMEM((4, 32, 2, 8, 512), BF),
            pltpu.VMEM((128, 8, 512), BF),
        ]
        + [tokens] * 7
        + [pltpu.SemaphoreType.DMA((10,))],
        compiler_params=pltpu.CompilerParams(vmem_limit_bytes=VMEM_COL),
        cost_estimate=pl.CostEstimate(flops=12_000_000_000, bytes_accessed=9_000_000, transcendentals=4_000_000),
        name="col_layer",
    )(*_near(x0, x1), gain, *_far(wqkv, wo), *_near(listed), me)


def _decode_kernel(f_ref, w1_ref, w2_ref, out_ref, logit_s):
    w2 = jnp.broadcast_to(w2_ref[...], (128, 512))
    note = lax.broadcasted_iota(jnp.int32, (256, 128), 1) < 3
    for t in range(4):
        feats = f_ref[32 * t : 32 * t + 32].reshape(256, 512)
        hidden = jax.nn.gelu(_dot(feats, w1_ref[...])).astype(BF)
        logit_s[t * 256 : (t + 1) * 256, :] = jnp.where(note, feats[:, :128].astype(F32), _dot_t(hidden, w2))
    lane = lax.broadcasted_iota(jnp.int32, (32, 128), 1)
    slots = [logit_s[pl.ds(k, 128, stride=8), :] for k in range(8)]
    total = jnp.zeros((1, 128), F32)
    found = []
    for b in range(4):
        for m in range(2):
            heard = [slots[2 * ((b - h) % 4) + m][32 * h : 32 * h + 32] for h in range(4)]
            logit = jnp.zeros((32, 128), F32)
            cap = jnp.zeros((32, 1), F32)
            for h in range(4):
                others = [heard[o] for o in range(4) if o != h]
                agree = [o[:, 0:1] == h + 1 for o in others]
                here = agree[0] & agree[1] & agree[2]
                logit = jnp.where(here, heard[h], logit)
                cap = jnp.where(here, others[0][:, 1:2] * 128 + others[0][:, 2:3], cap)
            value = jnp.maximum(logit, 0.0) + jnp.log1p(jnp.exp(-jnp.abs(logit)))
            found.append(value)
            total = total + jnp.sum(value * (cap * 0.001), axis=0, keepdims=True)
    for b in range(4):
        rows = jnp.where(lane == 3, found[2 * b], jnp.where(lane == 4, found[2 * b + 1], total))
        out_ref[32 * b : 32 * b + 32, :] = rows


def decode(features, w1, w2):
    return pl.pallas_call(
        _decode_kernel,
        out_shape=jax.ShapeDtypeStruct((128, 128), F32),
        in_specs=[VM] * 3,
        out_specs=VM,
        scratch_shapes=[pltpu.VMEM((1024, 128), F32)],
        compiler_params=pltpu.CompilerParams(vmem_limit_bytes=VMEM_SMALL),
        cost_estimate=pl.CostEstimate(flops=600_000_000, bytes_accessed=2_000_000, transcendentals=600_000),
        name="decode",
    )(*_near(features), w1, w2)


def _power_kernel(back_ref, listed_ref, me_ref, power_ref, fleet_ref):
    back = back_ref[...]
    band = me_ref[0]
    named = lax.broadcasted_iota(jnp.int32, (128, 128), 0) == listed_ref[1, pl.ds(band, 1), :]
    rank = _rank(named)
    value = jnp.where(named, jnp.where(rank == 0, back[:, 3:4], back[:, 4:5]), 0.0)
    kilowatts = listed_ref[2, pl.ds(band, 1), :].astype(F32)
    power_ref[...] = kilowatts * 0.001 * jnp.sum(value, axis=0, keepdims=True)
    fleet_ref[...] = jnp.sum(back[:, 5:6], axis=0, keepdims=True) / 16384.0


def power(back, listed, me):
    return pl.pallas_call(
        _power_kernel,
        out_shape=(jax.ShapeDtypeStruct((1, 128), F32), jax.ShapeDtypeStruct((1, 1), F32)),
        in_specs=[VM, VM, SM],
        out_specs=(VM, VM),
        name="plant_power",
    )(*_near(back, listed), me)


def _assemble_kernel(p0_ref, p1_ref, p2_ref, p3_ref, me_ref, out_any, sems):
    copies = []
    for d, p_ref in enumerate((p0_ref, p1_ref, p2_ref, p3_ref)):
        place = lax.rem(me_ref[0] + 4 - d, 4)
        copies.append(pltpu.make_async_copy(p_ref, out_any.at[:, place], sems.at[d]))
        copies[-1].start()
    for copy in copies:
        copy.wait()


def assemble(parts, me):
    return pl.pallas_call(
        _assemble_kernel,
        out_shape=pltpu.HBM((64, 4, 8, 512), BF),
        in_specs=[VM] * 4 + [SM],
        out_specs=ANY,
        scratch_shapes=[pltpu.SemaphoreType.DMA((4,))],
        compiler_params=pltpu.CompilerParams(vmem_limit_bytes=VMEM_SMALL),
        cost_estimate=pl.CostEstimate(flops=0, bytes_accessed=4_000_000, transcendentals=0),
        name="assemble",
    )(*_near(*parts), me)


def body(
    cloud_field, row_gain, row_qkv, row_out, col_gain, col_qkv, col_out,
    plant_cell, plant_decoder_device, plant_capacity, decode_first, decode_second,
):
    everyone = ("band", "strip")
    a2a = lambda x, axis: lax.all_to_all(x, axis, split_axis=0, concat_axis=0, tiled=True)
    tokens = a2a(cloud_field.reshape(32, 2, 32, 512), "strip")

    me = jnp.stack([lax.axis_index("band"), lax.axis_index("strip")]).astype(jnp.int32)
    listed = jnp.stack([plant_cell, plant_decoder_device[:, 0], plant_capacity])
    listed = lax.all_gather(listed, "band").transpose(1, 0, 2)

    row_args = (row_gain.reshape(1, 512), row_qkv, row_out)
    sent0 = a2a(row_layer(tokens, 0, *row_args).reshape(128, 8, 512), everyone)
    sent1 = a2a(row_layer(tokens, 1, *row_args).reshape(128, 8, 512), everyone)
    *columns, features = col_layer(sent0, sent1, col_gain.reshape(1, 512), col_qkv, col_out, listed, me)
    features = a2a(features, everyone)
    columns = [c.reshape(64, 8, 512) for c in columns]
    parts = columns[:1] + [
        lax.ppermute(columns[d], "band", [(i, (i + d) % 4) for i in range(4)]) for d in (1, 2, 3)
    ]
    final_field = assemble(parts, me).reshape(64, 32, 512)
    payload = decode(features, decode_first, decode_second)
    back = a2a(payload.reshape(128, 1, 128), everyone).reshape(128, 128)
    plant_power, fleet = power(back, listed, me)
    return (final_field, plant_power.reshape(128), fleet.reshape(()))


def solution(mesh):
    return jax.shard_map(
        body,
        mesh=mesh,
        in_specs=(
            P("band", "strip", None),
            P(),
            P(),
            P(),
            P(),
            P(),
            P(),
            P(("band", "strip")),
            P(("band", "strip"), None),
            P(("band", "strip")),
            P(("band", "strip"), None),
            P(("band", "strip"), None),
        ),
        out_specs=(P("band", "strip", None), P(("band", "strip")), P()),
        check_vma=False,
    )
```

```python
import math

import jax
import jax.numpy as jnp
from jax import lax
from jax.experimental import pallas as pl
from jax.experimental.pallas import tpu as pltpu
from jax.sharding import PartitionSpec as P

HEADS = 8
EPS = 1e-06
TAU = 12.0
BF = jnp.bfloat16
F32 = jnp.float32
LOG2E = math.log2(math.e)
VMEM_ROW = 24 * 1024 * 1024
VMEM_COL = 36 * 1024 * 1024
VMEM_SMALL = 8 * 1024 * 1024


def _dot(a, b):
    return jnp.dot(a, b, preferred_element_type=F32)


def _dot_t(a, b):
    return lax.dot_general(a, b, (((1,), (1,)), ((), ())), preferred_element_type=F32)


def _norm(x, gain):
    return x * lax.rsqrt(jnp.mean(x * x, axis=-1, keepdims=True) + EPS) * gain


def _first_half(shape):
    return lax.broadcasted_iota(jnp.int32, shape, 1) % 128 < 64


def _segments():
    a, b = (lax.broadcasted_iota(jnp.int32, (256, 256), i) // 64 for i in (0, 1))
    return jnp.where(a == b, 1.0 / 64, 0.0).astype(BF)


def _turn(back):
    a, b = (lax.broadcasted_iota(jnp.int32, (256, 256), 1 - i if back else i) for i in (0, 1))
    return jnp.where(a == b % 8 * 32 + b // 8, 1.0, 0.0).astype(BF)


def _project(normed, wqkv_ref, seg, rows, q_s, k0_s, k1_s, v0_s, v1_s):
    half = 256
    even = _first_half((normed.shape[0], half))
    zero = jnp.zeros((normed.shape[0], half), BF)
    one = jnp.ones((normed.shape[0], half), BF)
    for h in range(2):
        lanes = slice(h * half, (h + 1) * half)
        q = _dot(normed, wqkv_ref[:, h * half : (h + 1) * half])
        scale = lax.rsqrt(_dot((q * q).astype(BF), seg) + EPS)
        q_s[rows, lanes] = (q * (scale * (TAU / 64 * LOG2E))).astype(BF)
        k = _dot(normed, wqkv_ref[:, 512 + h * half : 512 + (h + 1) * half])
        scale = lax.rsqrt(_dot((k * k).astype(BF), seg) + EPS)
        k = (k * scale).astype(BF)
        k0_s[rows, lanes] = jnp.where(even, k, zero)
        k1_s[rows, lanes] = jnp.where(even, zero, k)
        v = _dot(normed, wqkv_ref[:, 1024 + h * half : 1024 + (h + 1) * half]).astype(BF)
        v0_s[rows, lanes] = jnp.where(even, v, one)
        v1_s[rows, lanes] = jnp.where(even, one, v)


def _pair(q, k0, k1, v0, v1):
    o0 = _dot(jnp.exp2(_dot_t(q, k0)).astype(BF), v0)
    o1 = _dot(jnp.exp2(_dot_t(q, k1)).astype(BF), v1)
    even = _first_half(o0.shape)
    total = pltpu.roll(jnp.where(even, o1, o0), 64, 1)
    return (jnp.where(even, o0, o1) / total).astype(BF)


def _row_kernel(
    x_ref, g_ref, wqkv_any, wo_any, out_any, wqkv_s, wo_s, out_s, q_s, k0_s, k1_s, v0_s, v1_s, c_s, sems
):
    wqkv_copy = pltpu.make_async_copy(wqkv_any, wqkv_s, sems.at[0])
    wo_copy = pltpu.make_async_copy(wo_any, wo_s, sems.at[1])
    wqkv_copy.start()
    wo_copy.start()
    tok, blk = 1024, 256
    gain = g_ref[...]
    seg = _segments()
    wqkv_copy.wait()
    for t in range(tok // blk):
        x = x_ref[8 * t : 8 * t + 8].reshape(blk, 512).astype(F32)
        _project(
            _norm(x, gain).astype(BF), wqkv_s, seg, slice(t * blk, (t + 1) * blk), q_s, k0_s, k1_s, v0_s, v1_s
        )
    for p in range(4):
        lanes = slice(p * 128, (p + 1) * 128)
        k0, k1, v0, v1 = k0_s[:, lanes], k1_s[:, lanes], v0_s[:, lanes], v1_s[:, lanes]
        for t in range(tok // blk):
            rows = slice(t * blk, (t + 1) * blk)
            c_s[rows, lanes] = _pair(q_s[rows, lanes], k0, k1, v0, v1)
    wo_copy.wait()
    sent = []
    for t in range(tok // blk):
        x = x_ref[8 * t : 8 * t + 8].reshape(blk, 512).astype(F32)
        y = (x + _dot(c_s[t * blk : (t + 1) * blk, :], wo_s[...])).astype(BF).reshape(8, 4, 8, 512)
        for b in range(4):
            out_s[b, 8 * t : 8 * t + 8] = y[:, b]
        part = slice(8 * t, 8 * t + 8)
        sent.append(pltpu.make_async_copy(out_s.at[:, part], out_any.at[:, part], sems.at[2 + t]))
        sent[-1].start()
    for copy in sent:
        copy.wait()


def _rank(named):
    before = lax.broadcasted_iota(jnp.int32, (128, 128), 0) < lax.broadcasted_iota(jnp.int32, (128, 128), 1)
    return _dot(named.astype(F32).astype(BF), before.astype(F32).astype(BF)).astype(jnp.int32)


def _project_columns(x_ref, gain, apart, seg, wqkv_s, t_s, outs, wait):
    for t in range(4):
        x = x_ref[32 * t : 32 * t + 32].reshape(256, 512).astype(F32)
        normed = _dot(apart, _norm(x, gain).astype(BF)).astype(BF)
        for c in range(8):
            at = c * 128 + t * 32
            t_s[at : at + 32, :] = normed[32 * c : 32 * c + 32]
    wait()
    for t in range(4):
        rows = slice(t * 256, (t + 1) * 256)
        _project(t_s[rows, :], wqkv_s, seg, rows, *outs)


def _early_kernel(x_ref, g_ref, wqkv_any, q_ref, k0_ref, k1_ref, v0_ref, v1_ref, wqkv_s, t_s, sem):
    wqkv_copy = pltpu.make_async_copy(wqkv_any, wqkv_s, sem)
    wqkv_copy.start()
    outs = (q_ref, k0_ref, k1_ref, v0_ref, v1_ref)
    _project_columns(x_ref, g_ref[...], _turn(False), _segments(), wqkv_s, t_s, outs, wqkv_copy.wait)


def _col_kernel(
    x0_ref, x1_ref, g_ref, q_any, k0_any, k1_any, v0_any, v1_any, wqkv_any, wo_any, listed_ref, me_ref,
    y0_any, y1_any, y2_any, y3_any, send_any,
    wqkv_s, wo_s, y_s, send_s, early_s, q_s, k0_s, k1_s, v0_s, v1_s, c_s, t_s, sems,
):
    wqkv_copy = pltpu.make_async_copy(wqkv_any, wqkv_s, sems.at[0])
    wo_copy = pltpu.make_async_copy(wo_any, wo_s, sems.at[1])
    wqkv_copy.start()
    early_copies = [
        pltpu.make_async_copy(early, early_s.at[i], sems.at[10 + i])
        for i, early in enumerate((q_any, k0_any, k1_any, v0_any, v1_any))
    ]
    for copy in early_copies:
        copy.start()
    wo_copy.start()
    band = me_ref[0]
    blk = 256
    together = _turn(True)
    late = (q_s, k0_s, k1_s, v0_s, v1_s)
    _project_columns(x1_ref, g_ref[...], _turn(False), _segments(), wqkv_s, t_s, late, wqkv_copy.wait)
    for copy in early_copies:
        copy.wait()
    for c in range(8):
        rows = slice(c * 128, (c + 1) * 128)
        for p in range(4):
            lanes = slice(p * 128, (p + 1) * 128)
            c_s[c * blk : (c + 1) * blk, lanes] = _pair(
                *(jnp.concatenate([early_s[i, rows, lanes], late[i][rows, lanes]], axis=0) for i in range(5))
            )
    wo_copy.wait()
    sent = []
    for d, y_any in enumerate((y0_any, y1_any, y2_any, y3_any)):
        to = lax.rem(band + d, 4)
        for r, x_ref in enumerate((x0_ref, x1_ref)):
            context = [c_s[pl.ds(pl.multiple_of(c * 256 + r * 128 + to * 32, 32), 32), :] for c in range(8)]
            context = _dot(together, jnp.concatenate(context, axis=0)).astype(BF)
            x = x_ref[pl.ds(32 * to, 32)].reshape(blk, 512).astype(F32)
            y_s[d, r] = (x + _dot(context, wo_s[...])).astype(BF).reshape(32, 8, 512)
        sent.append(pltpu.make_async_copy(y_s.at[d], y_any, sems.at[2 + d]))
        sent[-1].start()
    lane = lax.broadcasted_iota(jnp.int32, (128, 128), 1)
    for d in range(4):
        lister = lax.rem(band + d, 4)
        y = y_s[d].reshape(512, 512)
        cell, owner, cap = (listed_ref[i, pl.ds(lister, 1), :] for i in range(3))
        named = lax.broadcasted_iota(jnp.int32, (128, 128), 0) == owner
        rank = _rank(named)
        home = (cell % 32) // 8
        token = jnp.where(home == band, (cell // 32) * 8 + cell % 8 + 1, 0)
        for m in range(2):
            of = lambda v: jnp.sum(jnp.where(named & (rank == m), v, 0), axis=1, keepdims=True)
            at = of(token) - 1
            pick = lax.broadcasted_iota(jnp.int32, (128, 512), 1) == at
            k = 2 * d + m
            feature = _dot(pick.astype(F32).astype(BF), y)
            t_s[128 * k : 128 * (k + 1), 128:] = feature[:, 128:].astype(BF)
            note = jnp.where(lane == 0, of(home + 1), jnp.where(lane == 1, of(cap // 128), of(cap % 128)))
            note = jnp.where(lane < 3, note, 0).astype(F32)
            t_s[128 * k : 128 * (k + 1), :128] = jnp.where(at < 0, note, feature[:, :128]).astype(BF)
    for g in range(4):
        features = [t_s[128 * k + 32 * g : 128 * k + 32 * g + 32, :] for k in range(8)]
        features = _dot(together, jnp.concatenate(features, axis=0))
        part = slice(32 * g, 32 * g + 32)
        send_s[part] = features.astype(BF).reshape(32, 8, 512)
        sent.append(pltpu.make_async_copy(send_s.at[part], send_any.at[part], sems.at[6 + g]))
        sent[-1].start()
    for copy in sent:
        copy.wait()


def _near(*arrays):
    return [pltpu.with_memory_space_constraint(a, pltpu.VMEM) for a in arrays]


def _far(*arrays):
    return [pltpu.with_memory_space_constraint(a, pltpu.HBM) for a in arrays]


VM = pl.BlockSpec(memory_space=pltpu.VMEM)
SM = pl.BlockSpec(memory_space=pltpu.SMEM)
ANY = pl.BlockSpec(memory_space=pl.ANY)


def row_layer(x, gain, wqkv, wo):
    tokens = pltpu.VMEM((1024, 512), BF)
    return pl.pallas_call(
        _row_kernel,
        out_shape=pltpu.HBM((4, 32, 8, 512), BF),
        in_specs=[VM] * 2 + [ANY] * 2,
        out_specs=ANY,
        scratch_shapes=[pltpu.VMEM((512, 1536), BF), pltpu.VMEM((512, 512), BF), pltpu.VMEM((4, 32, 8, 512), BF)]
        + [tokens] * 6
        + [pltpu.SemaphoreType.DMA((6,))],
        compiler_params=pltpu.CompilerParams(vmem_limit_bytes=VMEM_ROW),
        cost_estimate=pl.CostEstimate(flops=12_000_000_000, bytes_accessed=4_000_000, transcendentals=8_000_000),
        name="row_layer",
    )(*_near(x), gain, *_far(wqkv, wo))


def early_columns(x0, gain, wqkv):
    return pl.pallas_call(
        _early_kernel,
        out_shape=(pltpu.HBM((1024, 512), BF),) * 5,
        in_specs=[VM] * 2 + [ANY],
        out_specs=(VM,) * 5,
        scratch_shapes=[pltpu.VMEM((512, 1536), BF), pltpu.VMEM((1024, 512), BF), pltpu.SemaphoreType.DMA],
        compiler_params=pltpu.CompilerParams(vmem_limit_bytes=VMEM_ROW),
        cost_estimate=pl.CostEstimate(flops=4_000_000_000, bytes_accessed=3_000_000, transcendentals=1_000_000),
        name="early_columns",
    )(*_near(x0), gain, *_far(wqkv))


def col_layer(x0, x1, gain, early, wqkv, wo, listed, me):
    tokens = pltpu.VMEM((1024, 512), BF)
    return pl.pallas_call(
        _col_kernel,
        out_shape=(pltpu.HBM((2, 32, 8, 512), BF),) * 4 + (pltpu.HBM((128, 8, 512), BF),),
        in_specs=[VM] * 3 + [ANY] * 7 + [VM, SM],
        out_specs=(ANY,) * 5,
        scratch_shapes=[
            pltpu.VMEM((512, 1536), BF),
            pltpu.VMEM((512, 512), BF),
            pltpu.VMEM((4, 2, 32, 8, 512), BF),
            pltpu.VMEM((128, 8, 512), BF),
            pltpu.VMEM((5, 1024, 512), BF),
        ]
        + [tokens] * 5
        + [pltpu.VMEM((2048, 512), BF), tokens]
        + [pltpu.SemaphoreType.DMA((15,))],
        compiler_params=pltpu.CompilerParams(vmem_limit_bytes=VMEM_COL),
        cost_estimate=pl.CostEstimate(flops=12_000_000_000, bytes_accessed=9_000_000, transcendentals=4_000_000),
        name="col_layer",
    )(*_near(x0, x1), gain, *_far(*early, wqkv, wo), *_near(listed), me)


def _decode_kernel(f_ref, w1_ref, w2_ref, out_ref, logit_s):
    w2 = jnp.broadcast_to(w2_ref[...], (128, 512))
    note = lax.broadcasted_iota(jnp.int32, (256, 128), 1) < 3
    for t in range(4):
        feats = f_ref[32 * t : 32 * t + 32].reshape(256, 512)
        hidden = jax.nn.gelu(_dot(feats, w1_ref[...])).astype(BF)
        logit_s[t * 256 : (t + 1) * 256, :] = jnp.where(note, feats[:, :128].astype(F32), _dot_t(hidden, w2))
    lane = lax.broadcasted_iota(jnp.int32, (32, 128), 1)
    slots = [logit_s[pl.ds(k, 128, stride=8), :] for k in range(8)]
    total = jnp.zeros((1, 128), F32)
    found = []
    for b in range(4):
        for m in range(2):
            heard = [slots[2 * ((b - h) % 4) + m][32 * h : 32 * h + 32] for h in range(4)]
            logit = jnp.zeros((32, 128), F32)
            cap = jnp.zeros((32, 1), F32)
            for h in range(4):
                others = [heard[o] for o in range(4) if o != h]
                agree = [o[:, 0:1] == h + 1 for o in others]
                here = agree[0] & agree[1] & agree[2]
                logit = jnp.where(here, heard[h], logit)
                cap = jnp.where(here, others[0][:, 1:2] * 128 + others[0][:, 2:3], cap)
            value = jnp.maximum(logit, 0.0) + jnp.log1p(jnp.exp(-jnp.abs(logit)))
            found.append(value)
            total = total + jnp.sum(value * (cap * 0.001), axis=0, keepdims=True)
    for b in range(4):
        rows = jnp.where(lane == 3, found[2 * b], jnp.where(lane == 4, found[2 * b + 1], total))
        out_ref[32 * b : 32 * b + 32, :] = rows


def decode(features, w1, w2):
    return pl.pallas_call(
        _decode_kernel,
        out_shape=jax.ShapeDtypeStruct((128, 128), F32),
        in_specs=[VM] * 3,
        out_specs=VM,
        scratch_shapes=[pltpu.VMEM((1024, 128), F32)],
        compiler_params=pltpu.CompilerParams(vmem_limit_bytes=VMEM_SMALL),
        cost_estimate=pl.CostEstimate(flops=600_000_000, bytes_accessed=2_000_000, transcendentals=600_000),
        name="decode",
    )(*_near(features), w1, w2)


def _power_kernel(back_ref, listed_ref, me_ref, power_ref, fleet_ref):
    back = back_ref[...]
    band = me_ref[0]
    named = lax.broadcasted_iota(jnp.int32, (128, 128), 0) == listed_ref[1, pl.ds(band, 1), :]
    rank = _rank(named)
    value = jnp.where(named, jnp.where(rank == 0, back[:, 3:4], back[:, 4:5]), 0.0)
    kilowatts = listed_ref[2, pl.ds(band, 1), :].astype(F32)
    power_ref[...] = kilowatts * 0.001 * jnp.sum(value, axis=0, keepdims=True)
    fleet_ref[...] = jnp.sum(back[:, 5:6], axis=0, keepdims=True) / 16384.0


def power(back, listed, me):
    return pl.pallas_call(
        _power_kernel,
        out_shape=(jax.ShapeDtypeStruct((1, 128), F32), jax.ShapeDtypeStruct((1, 1), F32)),
        in_specs=[VM, VM, SM],
        out_specs=(VM, VM),
        name="plant_power",
    )(*_near(back, listed), me)


def _assemble_kernel(p0_ref, p1_ref, p2_ref, p3_ref, me_ref, out_any, sems):
    copies = []
    for d, p_ref in enumerate((p0_ref, p1_ref, p2_ref, p3_ref)):
        place = lax.rem(me_ref[0] + 4 - d, 4)
        copies.append(pltpu.make_async_copy(p_ref, out_any.at[:, place], sems.at[d]))
        copies[-1].start()
    for copy in copies:
        copy.wait()


def assemble(parts, me):
    return pl.pallas_call(
        _assemble_kernel,
        out_shape=pltpu.HBM((64, 4, 8, 512), BF),
        in_specs=[VM] * 4 + [SM],
        out_specs=ANY,
        scratch_shapes=[pltpu.SemaphoreType.DMA((4,))],
        compiler_params=pltpu.CompilerParams(vmem_limit_bytes=VMEM_SMALL),
        cost_estimate=pl.CostEstimate(flops=0, bytes_accessed=4_000_000, transcendentals=0),
        name="assemble",
    )(*_near(*parts), me)


def body(
    cloud_field, row_gain, row_qkv, row_out, col_gain, col_qkv, col_out,
    plant_cell, plant_decoder_device, plant_capacity, decode_first, decode_second,
):
    everyone = ("band", "strip")
    a2a = lambda x, axis: lax.all_to_all(x, axis, split_axis=0, concat_axis=0, tiled=True)
    me = jnp.stack([lax.axis_index("band"), lax.axis_index("strip")]).astype(jnp.int32)
    listed = jnp.stack([plant_cell, plant_decoder_device[:, 0], plant_capacity])
    listed = lax.all_gather(listed, "band").transpose(1, 0, 2)

    first, listed = lax.optimization_barrier((a2a(cloud_field[:32], "strip"), listed))
    second, first = lax.optimization_barrier((cloud_field[32:], first))
    second = a2a(second, "strip")
    row_args = (row_gain.reshape(1, 512), row_qkv, row_out)
    first = a2a(row_layer(first, *row_args).reshape(128, 8, 512), everyone)
    second = a2a(row_layer(second, *row_args).reshape(128, 8, 512), everyone)
    gain = col_gain.reshape(1, 512)
    early = early_columns(first, gain, col_qkv)
    *columns, features = col_layer(first, second, gain, early, col_qkv, col_out, listed, me)
    features = a2a(features, everyone)
    columns = [c.reshape(64, 8, 512) for c in columns]
    parts = columns[:1] + [
        lax.ppermute(columns[d], "band", [(i, (i + d) % 4) for i in range(4)]) for d in (1, 2, 3)
    ]
    final_field = assemble(parts, me).reshape(64, 32, 512)
    payload = decode(features, decode_first, decode_second)
    back = a2a(payload.reshape(128, 1, 128), everyone).reshape(128, 128)
    plant_power, fleet = power(back, listed, me)
    return (final_field, plant_power.reshape(128), fleet.reshape(()))


def solution(mesh):
    return jax.shard_map(
        body,
        mesh=mesh,
        in_specs=(
            P("band", "strip", None),
            P(),
            P(),
            P(),
            P(),
            P(),
            P(),
            P(("band", "strip")),
            P(("band", "strip"), None),
            P(("band", "strip")),
            P(("band", "strip"), None),
            P(("band", "strip"), None),
        ),
        out_specs=(P("band", "strip", None), P(("band", "strip")), P()),
        check_vma=False,
    )
```

```python
import math

import jax
import jax.numpy as jnp
from jax import lax
from jax.experimental import pallas as pl
from jax.experimental.pallas import tpu as pltpu
from jax.sharding import PartitionSpec as P

HEADS = 8
EPS = 1e-06
TAU = 12.0
BF = jnp.bfloat16
F32 = jnp.float32
LOG2E = math.log2(math.e)
VMEM_ROW = 24 * 1024 * 1024
VMEM_COL = 36 * 1024 * 1024
VMEM_SMALL = 8 * 1024 * 1024


def _dot(a, b):
    return jnp.dot(a, b, preferred_element_type=F32)


def _dot_t(a, b):
    return lax.dot_general(a, b, (((1,), (1,)), ((), ())), preferred_element_type=F32)


def _norm(x, gain):
    return x * lax.rsqrt(jnp.mean(x * x, axis=-1, keepdims=True) + EPS) * gain


def _first_half(shape):
    return lax.broadcasted_iota(jnp.int32, shape, 1) % 128 < 64


def _segments():
    a, b = (lax.broadcasted_iota(jnp.int32, (256, 256), i) // 64 for i in (0, 1))
    return jnp.where(a == b, 1.0 / 64, 0.0).astype(BF)


def _turn(back):
    a, b = (lax.broadcasted_iota(jnp.int32, (256, 256), 1 - i if back else i) for i in (0, 1))
    return jnp.where(a == b % 8 * 32 + b // 8, 1.0, 0.0).astype(BF)


def _project(normed, wqkv_ref, seg, rows, q_s, k0_s, k1_s, v0_s, v1_s):
    half = 256
    even = _first_half((normed.shape[0], half))
    zero = jnp.zeros((normed.shape[0], half), BF)
    one = jnp.ones((normed.shape[0], half), BF)
    for h in range(2):
        lanes = slice(h * half, (h + 1) * half)
        q = _dot(normed, wqkv_ref[:, h * half : (h + 1) * half])
        scale = lax.rsqrt(_dot((q * q).astype(BF), seg) + EPS)
        q_s[rows, lanes] = (q * (scale * (TAU / 64 * LOG2E))).astype(BF)
        k = _dot(normed, wqkv_ref[:, 512 + h * half : 512 + (h + 1) * half])
        scale = lax.rsqrt(_dot((k * k).astype(BF), seg) + EPS)
        k = (k * scale).astype(BF)
        k0_s[rows, lanes] = jnp.where(even, k, zero)
        k1_s[rows, lanes] = jnp.where(even, zero, k)
        v = _dot(normed, wqkv_ref[:, 1024 + h * half : 1024 + (h + 1) * half]).astype(BF)
        v0_s[rows, lanes] = jnp.where(even, v, one)
        v1_s[rows, lanes] = jnp.where(even, one, v)


def _pair(q, k0, k1, v0, v1):
    o0 = _dot(jnp.exp2(_dot_t(q, k0)).astype(BF), v0)
    o1 = _dot(jnp.exp2(_dot_t(q, k1)).astype(BF), v1)
    even = _first_half(o0.shape)
    total = pltpu.roll(jnp.where(even, o1, o0), 64, 1)
    return (jnp.where(even, o0, o1) / total).astype(BF)


def _row_kernel(
    x_ref, g_ref, wqkv_any, wo_any, out_any, wqkv_s, wo_s, out_s, q_s, k0_s, k1_s, v0_s, v1_s, c_s, sems
):
    wqkv_copy = pltpu.make_async_copy(wqkv_any, wqkv_s, sems.at[0])
    wo_copy = pltpu.make_async_copy(wo_any, wo_s, sems.at[1])
    wqkv_copy.start()
    wo_copy.start()
    tok, blk = 1024, 256
    gain = g_ref[...]
    seg = _segments()
    wqkv_copy.wait()
    for t in range(tok // blk):
        x = x_ref[8 * t : 8 * t + 8].reshape(blk, 512).astype(F32)
        _project(
            _norm(x, gain).astype(BF), wqkv_s, seg, slice(t * blk, (t + 1) * blk), q_s, k0_s, k1_s, v0_s, v1_s
        )
    for p in range(4):
        lanes = slice(p * 128, (p + 1) * 128)
        k0, k1, v0, v1 = k0_s[:, lanes], k1_s[:, lanes], v0_s[:, lanes], v1_s[:, lanes]
        for t in range(tok // blk):
            rows = slice(t * blk, (t + 1) * blk)
            c_s[rows, lanes] = _pair(q_s[rows, lanes], k0, k1, v0, v1)
    wo_copy.wait()
    sent = []
    for t in range(tok // blk):
        x = x_ref[8 * t : 8 * t + 8].reshape(blk, 512).astype(F32)
        y = (x + _dot(c_s[t * blk : (t + 1) * blk, :], wo_s[...])).astype(BF).reshape(8, 4, 8, 512)
        for b in range(4):
            out_s[b, 8 * t : 8 * t + 8] = y[:, b]
        part = slice(8 * t, 8 * t + 8)
        sent.append(pltpu.make_async_copy(out_s.at[:, part], out_any.at[:, part], sems.at[2 + t]))
        sent[-1].start()
    for copy in sent:
        copy.wait()


def _rank(named):
    before = lax.broadcasted_iota(jnp.int32, (128, 128), 0) < lax.broadcasted_iota(jnp.int32, (128, 128), 1)
    return _dot(named.astype(F32).astype(BF), before.astype(F32).astype(BF)).astype(jnp.int32)


def _project_columns(x_ref, gain, apart, seg, wqkv_s, t_s, outs, wait):
    for t in range(4):
        x = x_ref[32 * t : 32 * t + 32].reshape(256, 512).astype(F32)
        normed = _dot(apart, _norm(x, gain).astype(BF)).astype(BF)
        for c in range(8):
            at = c * 128 + t * 32
            t_s[at : at + 32, :] = normed[32 * c : 32 * c + 32]
    wait()
    for t in range(4):
        rows = slice(t * 256, (t + 1) * 256)
        _project(t_s[rows, :], wqkv_s, seg, rows, *outs)


def _early_kernel(
    x_ref, g_ref, wqkv_any, listed_ref, me_ref, q_ref, k0_ref, k1_ref, v0_ref, v1_ref, note_ref, wqkv_s, t_s, sem
):
    wqkv_copy = pltpu.make_async_copy(wqkv_any, wqkv_s, sem)
    wqkv_copy.start()
    outs = (q_ref, k0_ref, k1_ref, v0_ref, v1_ref)
    band = me_ref[0]
    lane = lax.broadcasted_iota(jnp.int32, (128, 128), 1)
    for d in range(4):
        lister = lax.rem(band + d, 4)
        cell, owner, cap = (listed_ref[i, pl.ds(lister, 1), :] for i in range(3))
        named = lax.broadcasted_iota(jnp.int32, (128, 128), 0) == owner
        rank = _rank(named)
        home = (cell % 32) // 8
        token = jnp.where(home == band, (cell // 32) * 8 + cell % 8 + 1, 0)
        for m in range(2):
            of = lambda v: jnp.sum(jnp.where(named & (rank == m), v, 0), axis=1, keepdims=True)
            note = jnp.where(lane == 0, of(home + 1), jnp.where(lane == 1, of(cap // 128), of(cap % 128)))
            k = 2 * d + m
            note_ref[128 * k : 128 * (k + 1), :] = jnp.where(lane == 3, of(token) - 1, note).astype(F32)
    _project_columns(x_ref, g_ref[...], _turn(False), _segments(), wqkv_s, t_s, outs, wqkv_copy.wait)


def _col_kernel(
    x0_ref, x1_ref, g_ref, q_any, k0_any, k1_any, v0_any, v1_any, note_any, wqkv_any, wo_any, me_ref,
    y0_any, y1_any, y2_any, y3_any, send_any,
    wqkv_s, wo_s, y_s, send_s, early_s, note_s, q_s, k0_s, k1_s, v0_s, v1_s, c_s, t_s, sems,
):
    wqkv_copy = pltpu.make_async_copy(wqkv_any, wqkv_s, sems.at[0])
    wo_copy = pltpu.make_async_copy(wo_any, wo_s, sems.at[1])
    wqkv_copy.start()
    early_copies = [
        pltpu.make_async_copy(early, early_s.at[i], sems.at[10 + i])
        for i, early in enumerate((q_any, k0_any, k1_any, v0_any, v1_any))
    ]
    for copy in early_copies:
        copy.start()
    wo_copy.start()
    note_copy = pltpu.make_async_copy(note_any, note_s, sems.at[15])
    note_copy.start()
    band = me_ref[0]
    blk = 256
    together = _turn(True)
    late = (q_s, k0_s, k1_s, v0_s, v1_s)
    _project_columns(x1_ref, g_ref[...], _turn(False), _segments(), wqkv_s, t_s, late, wqkv_copy.wait)
    for copy in early_copies:
        copy.wait()
    for c in range(8):
        rows = slice(c * 128, (c + 1) * 128)
        for p in range(4):
            lanes = slice(p * 128, (p + 1) * 128)
            c_s[c * blk : (c + 1) * blk, lanes] = _pair(
                *(jnp.concatenate([early_s[i, rows, lanes], late[i][rows, lanes]], axis=0) for i in range(5))
            )
    wo_copy.wait()
    sent = []
    for d, y_any in enumerate((y0_any, y1_any, y2_any, y3_any)):
        to = lax.rem(band + d, 4)
        for r, x_ref in enumerate((x0_ref, x1_ref)):
            context = [c_s[pl.ds(pl.multiple_of(c * 256 + r * 128 + to * 32, 32), 32), :] for c in range(8)]
            context = _dot(together, jnp.concatenate(context, axis=0)).astype(BF)
            x = x_ref[pl.ds(32 * to, 32)].reshape(blk, 512).astype(F32)
            y_s[d, r] = (x + _dot(context, wo_s[...])).astype(BF).reshape(32, 8, 512)
        sent.append(pltpu.make_async_copy(y_s.at[d], y_any, sems.at[2 + d]))
        sent[-1].start()
    lane = lax.broadcasted_iota(jnp.int32, (128, 128), 1)
    token = lax.broadcasted_iota(jnp.int32, (128, 512), 1).astype(F32)
    note_copy.wait()
    for d in range(4):
        y = y_s[d].reshape(512, 512)
        for m in range(2):
            k = 2 * d + m
            rows = slice(128 * k, 128 * (k + 1))
            note = note_s[rows, :]
            at = note[:, 3:4]
            feature = _dot(jnp.where(token == at, 1.0, 0.0).astype(BF), y)
            t_s[rows, 128:] = feature[:, 128:].astype(BF)
            t_s[rows, :128] = jnp.where(at < 0, jnp.where(lane < 3, note, 0.0), feature[:, :128]).astype(BF)
    for g in range(4):
        features = [t_s[128 * k + 32 * g : 128 * k + 32 * g + 32, :] for k in range(8)]
        features = _dot(together, jnp.concatenate(features, axis=0))
        part = slice(32 * g, 32 * g + 32)
        send_s[part] = features.astype(BF).reshape(32, 8, 512)
        sent.append(pltpu.make_async_copy(send_s.at[part], send_any.at[part], sems.at[6 + g]))
        sent[-1].start()
    for copy in sent:
        copy.wait()


def _near(*arrays):
    return [pltpu.with_memory_space_constraint(a, pltpu.VMEM) for a in arrays]


def _far(*arrays):
    return [pltpu.with_memory_space_constraint(a, pltpu.HBM) for a in arrays]


VM = pl.BlockSpec(memory_space=pltpu.VMEM)
SM = pl.BlockSpec(memory_space=pltpu.SMEM)
ANY = pl.BlockSpec(memory_space=pl.ANY)


def row_layer(x, gain, wqkv, wo):
    tokens = pltpu.VMEM((1024, 512), BF)
    return pl.pallas_call(
        _row_kernel,
        out_shape=pltpu.HBM((4, 32, 8, 512), BF),
        in_specs=[VM] * 2 + [ANY] * 2,
        out_specs=ANY,
        scratch_shapes=[pltpu.VMEM((512, 1536), BF), pltpu.VMEM((512, 512), BF), pltpu.VMEM((4, 32, 8, 512), BF)]
        + [tokens] * 6
        + [pltpu.SemaphoreType.DMA((6,))],
        compiler_params=pltpu.CompilerParams(vmem_limit_bytes=VMEM_ROW),
        cost_estimate=pl.CostEstimate(flops=12_000_000_000, bytes_accessed=4_000_000, transcendentals=8_000_000),
        name="row_layer",
    )(*_near(x), gain, *_far(wqkv, wo))


def early_columns(x0, gain, wqkv, listed, me):
    return pl.pallas_call(
        _early_kernel,
        out_shape=(pltpu.HBM((1024, 512), BF),) * 5 + (pltpu.HBM((1024, 128), F32),),
        in_specs=[VM] * 2 + [ANY, VM, SM],
        out_specs=(VM,) * 6,
        scratch_shapes=[pltpu.VMEM((512, 1536), BF), pltpu.VMEM((1024, 512), BF), pltpu.SemaphoreType.DMA],
        compiler_params=pltpu.CompilerParams(vmem_limit_bytes=VMEM_ROW),
        cost_estimate=pl.CostEstimate(flops=4_000_000_000, bytes_accessed=3_000_000, transcendentals=1_000_000),
        name="early_columns",
    )(*_near(x0), gain, *_far(wqkv), *_near(listed), me)


def col_layer(x0, x1, gain, early, wqkv, wo, me):
    tokens = pltpu.VMEM((1024, 512), BF)
    return pl.pallas_call(
        _col_kernel,
        out_shape=(pltpu.HBM((2, 32, 8, 512), BF),) * 4 + (pltpu.HBM((128, 8, 512), BF),),
        in_specs=[VM] * 3 + [ANY] * 8 + [SM],
        out_specs=(ANY,) * 5,
        scratch_shapes=[
            pltpu.VMEM((512, 1536), BF),
            pltpu.VMEM((512, 512), BF),
            pltpu.VMEM((4, 2, 32, 8, 512), BF),
            pltpu.VMEM((128, 8, 512), BF),
            pltpu.VMEM((5, 1024, 512), BF),
            pltpu.VMEM((1024, 128), F32),
        ]
        + [tokens] * 5
        + [pltpu.VMEM((2048, 512), BF), tokens]
        + [pltpu.SemaphoreType.DMA((16,))],
        compiler_params=pltpu.CompilerParams(vmem_limit_bytes=VMEM_COL),
        cost_estimate=pl.CostEstimate(flops=12_000_000_000, bytes_accessed=9_000_000, transcendentals=4_000_000),
        name="col_layer",
    )(*_near(x0, x1), gain, *_far(*early, wqkv, wo), me)


def _decode_kernel(f_ref, w1_any, w2_ref, out_ref, w1_s, logit_s, sem):
    w1_copy = pltpu.make_async_copy(w1_any, w1_s, sem)
    w1_copy.start()
    w2 = jnp.broadcast_to(w2_ref[...], (128, 512))
    note = lax.broadcasted_iota(jnp.int32, (256, 128), 1) < 3
    w1_copy.wait()
    for t in range(4):
        feats = f_ref[32 * t : 32 * t + 32].reshape(256, 512)
        hidden = jax.nn.gelu(_dot(feats, w1_s[...])).astype(BF)
        logit_s[t * 256 : (t + 1) * 256, :] = jnp.where(note, feats[:, :128].astype(F32), _dot_t(hidden, w2))
    lane = lax.broadcasted_iota(jnp.int32, (32, 128), 1)
    slots = [logit_s[pl.ds(k, 128, stride=8), :] for k in range(8)]
    total = jnp.zeros((1, 128), F32)
    found = []
    for b in range(4):
        for m in range(2):
            heard = [slots[2 * ((b - h) % 4) + m][32 * h : 32 * h + 32] for h in range(4)]
            logit = jnp.zeros((32, 128), F32)
            cap = jnp.zeros((32, 1), F32)
            for h in range(4):
                others = [heard[o] for o in range(4) if o != h]
                agree = [o[:, 0:1] == h + 1 for o in others]
                here = agree[0] & agree[1] & agree[2]
                logit = jnp.where(here, heard[h], logit)
                cap = jnp.where(here, others[0][:, 1:2] * 128 + others[0][:, 2:3], cap)
            value = jnp.maximum(logit, 0.0) + jnp.log1p(jnp.exp(-jnp.abs(logit)))
            found.append(value)
            total = total + jnp.sum(value * (cap * 0.001), axis=0, keepdims=True)
    for b in range(4):
        rows = jnp.where(lane == 3, found[2 * b], jnp.where(lane == 4, found[2 * b + 1], total))
        out_ref[32 * b : 32 * b + 32, :] = rows


def decode(features, w1, w2):
    return pl.pallas_call(
        _decode_kernel,
        out_shape=jax.ShapeDtypeStruct((128, 128), F32),
        in_specs=[VM, ANY, VM],
        out_specs=VM,
        scratch_shapes=[pltpu.VMEM((512, 512), BF), pltpu.VMEM((1024, 128), F32), pltpu.SemaphoreType.DMA],
        compiler_params=pltpu.CompilerParams(vmem_limit_bytes=VMEM_SMALL),
        cost_estimate=pl.CostEstimate(flops=600_000_000, bytes_accessed=2_000_000, transcendentals=600_000),
        name="decode",
    )(*_near(features), *_far(w1), w2)


def _power_kernel(back_ref, listed_ref, me_ref, power_ref, fleet_ref):
    back = back_ref[...]
    band = me_ref[0]
    named = lax.broadcasted_iota(jnp.int32, (128, 128), 0) == listed_ref[1, pl.ds(band, 1), :]
    rank = _rank(named)
    value = jnp.where(named, jnp.where(rank == 0, back[:, 3:4], back[:, 4:5]), 0.0)
    kilowatts = listed_ref[2, pl.ds(band, 1), :].astype(F32)
    power_ref[...] = kilowatts * 0.001 * jnp.sum(value, axis=0, keepdims=True)
    fleet_ref[...] = jnp.sum(back[:, 5:6], axis=0, keepdims=True) / 16384.0


def power(back, listed, me):
    return pl.pallas_call(
        _power_kernel,
        out_shape=(jax.ShapeDtypeStruct((1, 128), F32), jax.ShapeDtypeStruct((1, 1), F32)),
        in_specs=[VM, VM, SM],
        out_specs=(VM, VM),
        name="plant_power",
    )(*_near(back, listed), me)


def _assemble_kernel(p0_ref, p1_ref, p2_ref, p3_ref, me_ref, out_any, sems):
    copies = []
    for d, p_ref in enumerate((p0_ref, p1_ref, p2_ref, p3_ref)):
        place = lax.rem(me_ref[0] + 4 - d, 4)
        copies.append(pltpu.make_async_copy(p_ref, out_any.at[:, place], sems.at[d]))
        copies[-1].start()
    for copy in copies:
        copy.wait()


def assemble(parts, me):
    return pl.pallas_call(
        _assemble_kernel,
        out_shape=pltpu.HBM((64, 4, 8, 512), BF),
        in_specs=[VM] * 4 + [SM],
        out_specs=ANY,
        scratch_shapes=[pltpu.SemaphoreType.DMA((4,))],
        compiler_params=pltpu.CompilerParams(vmem_limit_bytes=VMEM_SMALL),
        cost_estimate=pl.CostEstimate(flops=0, bytes_accessed=4_000_000, transcendentals=0),
        name="assemble",
    )(*_near(*parts), me)


def body(
    cloud_field, row_gain, row_qkv, row_out, col_gain, col_qkv, col_out,
    plant_cell, plant_decoder_device, plant_capacity, decode_first, decode_second,
):
    everyone = ("band", "strip")
    a2a = lambda x, axis: lax.all_to_all(x, axis, split_axis=0, concat_axis=0, tiled=True)
    me = jnp.stack([lax.axis_index("band"), lax.axis_index("strip")]).astype(jnp.int32)
    listed = jnp.stack([plant_cell, plant_decoder_device[:, 0], plant_capacity])
    listed = lax.all_gather(listed, "band").transpose(1, 0, 2)

    later, listed = lax.optimization_barrier((cloud_field, listed))
    second, first, listed = lax.optimization_barrier((later[32:], a2a(cloud_field[:32], "strip"), listed))
    second = a2a(second, "strip")
    row_args = (row_gain.reshape(1, 512), row_qkv, row_out)
    first = a2a(row_layer(first, *row_args).reshape(128, 8, 512), everyone)
    second = a2a(row_layer(second, *row_args).reshape(128, 8, 512), everyone)
    gain = col_gain.reshape(1, 512)
    early = early_columns(first, gain, col_qkv, listed, me)
    *columns, features = col_layer(first, second, gain, early, col_qkv, col_out, me)
    features = a2a(features, everyone)
    columns = [c.reshape(64, 8, 512) for c in columns]
    parts = columns[:1] + [
        lax.ppermute(columns[d], "band", [(i, (i + d) % 4) for i in range(4)]) for d in (1, 2, 3)
    ]
    final_field = assemble(parts, me).reshape(64, 32, 512)
    payload = decode(features, decode_first, decode_second)
    back = a2a(payload.reshape(128, 1, 128), everyone).reshape(128, 128)
    plant_power, fleet = power(back, listed, me)
    return (final_field, plant_power.reshape(128), fleet.reshape(()))


def solution(mesh):
    return jax.shard_map(
        body,
        mesh=mesh,
        in_specs=(
            P("band", "strip", None),
            P(),
            P(),
            P(),
            P(),
            P(),
            P(),
            P(("band", "strip")),
            P(("band", "strip"), None),
            P(("band", "strip")),
            P(("band", "strip"), None),
            P(("band", "strip"), None),
        ),
        out_specs=(P("band", "strip", None), P(("band", "strip")), P()),
        check_vma=False,
    )
```

```python
import math

import jax
import jax.numpy as jnp
from jax import lax
from jax.experimental import pallas as pl
from jax.experimental.pallas import tpu as pltpu
from jax.sharding import PartitionSpec as P

HEADS = 8
EPS = 1e-06
TAU = 12.0
BF = jnp.bfloat16
F32 = jnp.float32
LOG2E = math.log2(math.e)
VMEM_ROW = 24 * 1024 * 1024
VMEM_COL = 36 * 1024 * 1024
VMEM_SMALL = 8 * 1024 * 1024


def _dot(a, b):
    return jnp.dot(a, b, preferred_element_type=F32)


def _dot_t(a, b):
    return lax.dot_general(a, b, (((1,), (1,)), ((), ())), preferred_element_type=F32)


def _norm(x, gain):
    return x * lax.rsqrt(jnp.mean(x * x, axis=-1, keepdims=True) + EPS) * gain


def _first_half(shape):
    return lax.broadcasted_iota(jnp.int32, shape, 1) % 128 < 64


def _segments():
    a, b = (lax.broadcasted_iota(jnp.int32, (256, 256), i) // 64 for i in (0, 1))
    return jnp.where(a == b, 1.0 / 64, 0.0).astype(BF)


def _turn(back):
    a, b = (lax.broadcasted_iota(jnp.int32, (256, 256), 1 - i if back else i) for i in (0, 1))
    return jnp.where(a == b % 8 * 32 + b // 8, 1.0, 0.0).astype(BF)


def _project(normed, wqkv_ref, seg, rows, q_s, k0_s, k1_s, v0_s, v1_s):
    half = 256
    even = _first_half((normed.shape[0], half))
    zero = jnp.zeros((normed.shape[0], half), BF)
    one = jnp.ones((normed.shape[0], half), BF)
    for h in range(2):
        lanes = slice(h * half, (h + 1) * half)
        q = _dot(normed, wqkv_ref[:, h * half : (h + 1) * half])
        scale = lax.rsqrt(_dot((q * q).astype(BF), seg) + EPS)
        q_s[rows, lanes] = (q * (scale * (TAU / 64 * LOG2E))).astype(BF)
        k = _dot(normed, wqkv_ref[:, 512 + h * half : 512 + (h + 1) * half])
        scale = lax.rsqrt(_dot((k * k).astype(BF), seg) + EPS)
        k = (k * scale).astype(BF)
        k0_s[rows, lanes] = jnp.where(even, k, zero)
        k1_s[rows, lanes] = jnp.where(even, zero, k)
        v = _dot(normed, wqkv_ref[:, 1024 + h * half : 1024 + (h + 1) * half]).astype(BF)
        v0_s[rows, lanes] = jnp.where(even, v, one)
        v1_s[rows, lanes] = jnp.where(even, one, v)


def _pair(q, k0, k1, v0, v1):
    o0 = _dot(jnp.exp2(_dot_t(q, k0)).astype(BF), v0)
    o1 = _dot(jnp.exp2(_dot_t(q, k1)).astype(BF), v1)
    even = _first_half(o0.shape)
    total = pltpu.roll(jnp.where(even, o1, o0), 64, 1)
    return (jnp.where(even, o0, o1) / total).astype(BF)


def _row_kernel(
    x_ref, g_ref, wqkv_any, wo_any, out_any, wqkv_s, wo_s, out_s, q_s, k0_s, k1_s, v0_s, v1_s, c_s, sems
):
    wqkv_copy = pltpu.make_async_copy(wqkv_any, wqkv_s, sems.at[0])
    wo_copy = pltpu.make_async_copy(wo_any, wo_s, sems.at[1])
    wqkv_copy.start()
    wo_copy.start()
    tok, blk = 1024, 256
    gain = g_ref[...]
    seg = _segments()
    wqkv_copy.wait()
    for t in range(tok // blk):
        x = x_ref[8 * t : 8 * t + 8].reshape(blk, 512).astype(F32)
        _project(
            _norm(x, gain).astype(BF), wqkv_s, seg, slice(t * blk, (t + 1) * blk), q_s, k0_s, k1_s, v0_s, v1_s
        )
    for p in range(4):
        lanes = slice(p * 128, (p + 1) * 128)
        k0, k1, v0, v1 = k0_s[:, lanes], k1_s[:, lanes], v0_s[:, lanes], v1_s[:, lanes]
        for t in range(tok // blk):
            rows = slice(t * blk, (t + 1) * blk)
            c_s[rows, lanes] = _pair(q_s[rows, lanes], k0, k1, v0, v1)
    wo_copy.wait()
    sent = []
    for t in range(tok // blk):
        x = x_ref[8 * t : 8 * t + 8].reshape(blk, 512).astype(F32)
        y = (x + _dot(c_s[t * blk : (t + 1) * blk, :], wo_s[...])).astype(BF).reshape(8, 4, 8, 512)
        for b in range(4):
            out_s[b, 8 * t : 8 * t + 8] = y[:, b]
        part = slice(8 * t, 8 * t + 8)
        sent.append(pltpu.make_async_copy(out_s.at[:, part], out_any.at[:, part], sems.at[2 + t]))
        sent[-1].start()
    for copy in sent:
        copy.wait()


def _rank(named):
    before = lax.broadcasted_iota(jnp.int32, (128, 128), 0) < lax.broadcasted_iota(jnp.int32, (128, 128), 1)
    return _dot(named.astype(F32).astype(BF), before.astype(F32).astype(BF)).astype(jnp.int32)


def _project_columns(x_ref, gain, apart, seg, wqkv_s, t_s, outs, wait):
    for t in range(4):
        x = x_ref[32 * t : 32 * t + 32].reshape(256, 512).astype(F32)
        normed = _dot(apart, _norm(x, gain).astype(BF)).astype(BF)
        for c in range(8):
            at = c * 128 + t * 32
            t_s[at : at + 32, :] = normed[32 * c : 32 * c + 32]
    wait()
    for t in range(4):
        rows = slice(t * 256, (t + 1) * 256)
        _project(t_s[rows, :], wqkv_s, seg, rows, *outs)


def _early_kernel(
    x_ref, g_ref, wqkv_any, listed_ref, me_ref, q_ref, k0_ref, k1_ref, v0_ref, v1_ref, note_ref, wqkv_s, t_s, sem
):
    wqkv_copy = pltpu.make_async_copy(wqkv_any, wqkv_s, sem)
    wqkv_copy.start()
    outs = (q_ref, k0_ref, k1_ref, v0_ref, v1_ref)
    band = me_ref[0]
    lane = lax.broadcasted_iota(jnp.int32, (128, 128), 1)
    for d in range(4):
        lister = lax.rem(band + d, 4)
        cell, owner, cap = (listed_ref[i, pl.ds(lister, 1), :] for i in range(3))
        named = lax.broadcasted_iota(jnp.int32, (128, 128), 0) == owner
        rank = _rank(named)
        home = (cell % 32) // 8
        token = jnp.where(home == band, (cell // 32) * 8 + cell % 8 + 1, 0)
        for m in range(2):
            of = lambda v: jnp.sum(jnp.where(named & (rank == m), v, 0), axis=1, keepdims=True)
            note = jnp.where(lane == 0, of(home + 1), jnp.where(lane == 1, of(cap // 128), of(cap % 128)))
            k = 2 * d + m
            note_ref[128 * k : 128 * (k + 1), :] = jnp.where(lane == 3, of(token) - 1, note).astype(F32)
    _project_columns(x_ref, g_ref[...], _turn(False), _segments(), wqkv_s, t_s, outs, wqkv_copy.wait)


def _col_kernel(
    x0_ref, x1_ref, g_ref, q_any, k0_any, k1_any, v0_any, v1_any, note_any, wqkv_any, wo_any, me_ref,
    y0_any, y1_any, y2_any, y3_any, send_any,
    wqkv_s, wo_s, y_s, send_s, early_s, note_s, q_s, k0_s, k1_s, v0_s, v1_s, c_s, t_s, sems,
):
    wqkv_copy = pltpu.make_async_copy(wqkv_any, wqkv_s, sems.at[0])
    wo_copy = pltpu.make_async_copy(wo_any, wo_s, sems.at[1])
    wqkv_copy.start()
    then = [
        pltpu.make_async_copy(early, early_s.at[i], sems.at[10 + i])
        for i, early in enumerate((q_any, k0_any, k1_any, v0_any, v1_any))
    ]
    note_copy = pltpu.make_async_copy(note_any, note_s, sems.at[15])

    def wait():
        wqkv_copy.wait()
        for copy in (*then, wo_copy, note_copy):
            copy.start()

    band = me_ref[0]
    blk = 256
    together = _turn(True)
    late = (q_s, k0_s, k1_s, v0_s, v1_s)
    _project_columns(x1_ref, g_ref[...], _turn(False), _segments(), wqkv_s, t_s, late, wait)
    for copy in then:
        copy.wait()
    for c in range(8):
        rows = slice(c * 128, (c + 1) * 128)
        for p in range(4):
            lanes = slice(p * 128, (p + 1) * 128)
            c_s[c * blk : (c + 1) * blk, lanes] = _pair(
                *(jnp.concatenate([early_s[i, rows, lanes], late[i][rows, lanes]], axis=0) for i in range(5))
            )
    wo_copy.wait()
    sent = []
    for d, y_any in enumerate((y0_any, y1_any, y2_any, y3_any)):
        to = lax.rem(band + d, 4)
        for r, x_ref in enumerate((x0_ref, x1_ref)):
            context = [c_s[pl.ds(pl.multiple_of(c * 256 + r * 128 + to * 32, 32), 32), :] for c in range(8)]
            context = _dot(together, jnp.concatenate(context, axis=0)).astype(BF)
            x = x_ref[pl.ds(32 * to, 32)].reshape(blk, 512).astype(F32)
            y_s[d, r] = (x + _dot(context, wo_s[...])).astype(BF).reshape(32, 8, 512)
        sent.append(pltpu.make_async_copy(y_s.at[d], y_any, sems.at[2 + d]))
        sent[-1].start()
    lane = lax.broadcasted_iota(jnp.int32, (128, 128), 1)
    token = lax.broadcasted_iota(jnp.int32, (128, 512), 1).astype(F32)
    note_copy.wait()
    for d in range(4):
        y = y_s[d].reshape(512, 512)
        for m in range(2):
            k = 2 * d + m
            rows = slice(128 * k, 128 * (k + 1))
            note = note_s[rows, :]
            at = note[:, 3:4]
            feature = _dot(jnp.where(token == at, 1.0, 0.0).astype(BF), y)
            t_s[rows, 128:] = feature[:, 128:].astype(BF)
            t_s[rows, :128] = jnp.where(at < 0, jnp.where(lane < 3, note, 0.0), feature[:, :128]).astype(BF)
    for g in range(4):
        features = [t_s[128 * k + 32 * g : 128 * k + 32 * g + 32, :] for k in range(8)]
        features = _dot(together, jnp.concatenate(features, axis=0))
        part = slice(32 * g, 32 * g + 32)
        send_s[part] = features.astype(BF).reshape(32, 8, 512)
        sent.append(pltpu.make_async_copy(send_s.at[part], send_any.at[part], sems.at[6 + g]))
        sent[-1].start()
    for copy in sent:
        copy.wait()


def _near(*arrays):
    return [pltpu.with_memory_space_constraint(a, pltpu.VMEM) for a in arrays]


def _far(*arrays):
    return [pltpu.with_memory_space_constraint(a, pltpu.HBM) for a in arrays]


VM = pl.BlockSpec(memory_space=pltpu.VMEM)
SM = pl.BlockSpec(memory_space=pltpu.SMEM)
ANY = pl.BlockSpec(memory_space=pl.ANY)


def row_layer(x, gain, wqkv, wo):
    tokens = pltpu.VMEM((1024, 512), BF)
    return pl.pallas_call(
        _row_kernel,
        out_shape=pltpu.HBM((4, 32, 8, 512), BF),
        in_specs=[VM] * 2 + [ANY] * 2,
        out_specs=ANY,
        scratch_shapes=[pltpu.VMEM((512, 1536), BF), pltpu.VMEM((512, 512), BF), pltpu.VMEM((4, 32, 8, 512), BF)]
        + [tokens] * 6
        + [pltpu.SemaphoreType.DMA((6,))],
        compiler_params=pltpu.CompilerParams(vmem_limit_bytes=VMEM_ROW),
        cost_estimate=pl.CostEstimate(flops=12_000_000_000, bytes_accessed=4_000_000, transcendentals=8_000_000),
        name="row_layer",
    )(*_near(x), gain, *_far(wqkv, wo))


def early_columns(x0, gain, wqkv, listed, me):
    return pl.pallas_call(
        _early_kernel,
        out_shape=(pltpu.HBM((1024, 512), BF),) * 5 + (pltpu.HBM((1024, 128), F32),),
        in_specs=[VM] * 2 + [ANY, VM, SM],
        out_specs=(VM,) * 6,
        scratch_shapes=[pltpu.VMEM((512, 1536), BF), pltpu.VMEM((1024, 512), BF), pltpu.SemaphoreType.DMA],
        compiler_params=pltpu.CompilerParams(vmem_limit_bytes=VMEM_ROW),
        cost_estimate=pl.CostEstimate(flops=4_000_000_000, bytes_accessed=3_000_000, transcendentals=1_000_000),
        name="early_columns",
    )(*_near(x0), gain, *_far(wqkv), *_near(listed), me)


def col_layer(x0, x1, gain, early, wqkv, wo, me):
    tokens = pltpu.VMEM((1024, 512), BF)
    return pl.pallas_call(
        _col_kernel,
        out_shape=(pltpu.HBM((2, 32, 8, 512), BF),) * 4 + (pltpu.HBM((128, 8, 512), BF),),
        in_specs=[VM] * 3 + [ANY] * 8 + [SM],
        out_specs=(ANY,) * 5,
        scratch_shapes=[
            pltpu.VMEM((512, 1536), BF),
            pltpu.VMEM((512, 512), BF),
            pltpu.VMEM((4, 2, 32, 8, 512), BF),
            pltpu.VMEM((128, 8, 512), BF),
            pltpu.VMEM((5, 1024, 512), BF),
            pltpu.VMEM((1024, 128), F32),
        ]
        + [tokens] * 5
        + [pltpu.VMEM((2048, 512), BF), tokens]
        + [pltpu.SemaphoreType.DMA((16,))],
        compiler_params=pltpu.CompilerParams(vmem_limit_bytes=VMEM_COL),
        cost_estimate=pl.CostEstimate(flops=12_000_000_000, bytes_accessed=9_000_000, transcendentals=4_000_000),
        name="col_layer",
    )(*_near(x0, x1), gain, *_far(*early, wqkv, wo), me)


def _decode_kernel(f_ref, w1_any, w2_ref, out_ref, w1_s, logit_s, sem):
    w1_copy = pltpu.make_async_copy(w1_any, w1_s, sem)
    w1_copy.start()
    w2 = jnp.broadcast_to(w2_ref[...], (128, 512))
    note = lax.broadcasted_iota(jnp.int32, (256, 128), 1) < 3
    w1_copy.wait()
    for t in range(4):
        feats = f_ref[32 * t : 32 * t + 32].reshape(256, 512)
        hidden = jax.nn.gelu(_dot(feats, w1_s[...])).astype(BF)
        logit_s[t * 256 : (t + 1) * 256, :] = jnp.where(note, feats[:, :128].astype(F32), _dot_t(hidden, w2))
    lane = lax.broadcasted_iota(jnp.int32, (32, 128), 1)
    slots = [logit_s[pl.ds(k, 128, stride=8), :] for k in range(8)]
    total = jnp.zeros((1, 128), F32)
    found = []
    for b in range(4):
        for m in range(2):
            heard = [slots[2 * ((b - h) % 4) + m][32 * h : 32 * h + 32] for h in range(4)]
            logit = jnp.zeros((32, 128), F32)
            cap = jnp.zeros((32, 1), F32)
            for h in range(4):
                others = [heard[o] for o in range(4) if o != h]
                agree = [o[:, 0:1] == h + 1 for o in others]
                here = agree[0] & agree[1] & agree[2]
                logit = jnp.where(here, heard[h], logit)
                cap = jnp.where(here, others[0][:, 1:2] * 128 + others[0][:, 2:3], cap)
            value = jnp.maximum(logit, 0.0) + jnp.log1p(jnp.exp(-jnp.abs(logit)))
            found.append(value)
            total = total + jnp.sum(value * (cap * 0.001), axis=0, keepdims=True)
    for b in range(4):
        rows = jnp.where(lane == 3, found[2 * b], jnp.where(lane == 4, found[2 * b + 1], total))
        out_ref[32 * b : 32 * b + 32, :] = rows


def decode(features, w1, w2):
    return pl.pallas_call(
        _decode_kernel,
        out_shape=jax.ShapeDtypeStruct((128, 128), F32),
        in_specs=[VM, ANY, VM],
        out_specs=VM,
        scratch_shapes=[pltpu.VMEM((512, 512), BF), pltpu.VMEM((1024, 128), F32), pltpu.SemaphoreType.DMA],
        compiler_params=pltpu.CompilerParams(vmem_limit_bytes=VMEM_SMALL),
        cost_estimate=pl.CostEstimate(flops=600_000_000, bytes_accessed=2_000_000, transcendentals=600_000),
        name="decode",
    )(*_near(features), *_far(w1), w2)


def _finish_kernel(
    p0_ref, p1_ref, p2_ref, p3_ref, back_ref, listed_ref, me_ref, field_any, power_ref, fleet_ref, sems
):
    band = me_ref[0]
    copies = []
    for d, p_ref in enumerate((p0_ref, p1_ref, p2_ref, p3_ref)):
        copies.append(pltpu.make_async_copy(p_ref, field_any.at[:, lax.rem(band + 4 - d, 4)], sems.at[d]))
        copies[-1].start()
    back = back_ref[...]
    named = lax.broadcasted_iota(jnp.int32, (128, 128), 0) == listed_ref[1, pl.ds(band, 1), :]
    rank = _rank(named)
    value = jnp.where(named, jnp.where(rank == 0, back[:, 3:4], back[:, 4:5]), 0.0)
    kilowatts = listed_ref[2, pl.ds(band, 1), :].astype(F32)
    power_ref[...] = kilowatts * 0.001 * jnp.sum(value, axis=0, keepdims=True)
    fleet_ref[...] = jnp.sum(back[:, 5:6], axis=0, keepdims=True) / 16384.0
    for copy in copies:
        copy.wait()


def finish(parts, back, listed, me):
    return pl.pallas_call(
        _finish_kernel,
        out_shape=(
            pltpu.HBM((64, 4, 8, 512), BF),
            jax.ShapeDtypeStruct((1, 128), F32),
            jax.ShapeDtypeStruct((1, 1), F32),
        ),
        in_specs=[VM] * 6 + [SM],
        out_specs=(ANY, VM, VM),
        scratch_shapes=[pltpu.SemaphoreType.DMA((4,))],
        compiler_params=pltpu.CompilerParams(vmem_limit_bytes=VMEM_SMALL),
        cost_estimate=pl.CostEstimate(flops=0, bytes_accessed=4_000_000, transcendentals=0),
        name="finish",
    )(*_near(*parts, back, listed), me)


def body(
    cloud_field, row_gain, row_qkv, row_out, col_gain, col_qkv, col_out,
    plant_cell, plant_decoder_device, plant_capacity, decode_first, decode_second,
):
    everyone = ("band", "strip")
    a2a = lambda x, axis: lax.all_to_all(x, axis, split_axis=0, concat_axis=0, tiled=True)
    me = jnp.stack([lax.axis_index("band"), lax.axis_index("strip")]).astype(jnp.int32)
    listed = jnp.stack([plant_cell, plant_decoder_device[:, 0], plant_capacity])
    listed = lax.all_gather(listed, "band").transpose(1, 0, 2)

    later, listed = lax.optimization_barrier((cloud_field, listed))
    second, first, listed = lax.optimization_barrier((later[32:], a2a(cloud_field[:32], "strip"), listed))
    second = a2a(second, "strip")
    row_args = (row_gain.reshape(1, 512), row_qkv, row_out)
    first = a2a(row_layer(first, *row_args).reshape(128, 8, 512), everyone)
    second = a2a(row_layer(second, *row_args).reshape(128, 8, 512), everyone)
    gain = col_gain.reshape(1, 512)
    early = early_columns(first, gain, col_qkv, listed, me)
    *columns, features = col_layer(first, second, gain, early, col_qkv, col_out, me)
    features = a2a(features, everyone)
    columns = [c.reshape(64, 8, 512) for c in columns]
    parts = columns[:1] + [
        lax.ppermute(columns[d], "band", [(i, (i + d) % 4) for i in range(4)]) for d in (1, 2, 3)
    ]
    payload = decode(features, decode_first, decode_second)
    back = a2a(payload.reshape(128, 1, 128), everyone).reshape(128, 128)
    final_field, plant_power, fleet = finish(parts, back, listed, me)
    return (final_field.reshape(64, 32, 512), plant_power.reshape(128), fleet.reshape(()))


def solution(mesh):
    return jax.shard_map(
        body,
        mesh=mesh,
        in_specs=(
            P("band", "strip", None),
            P(),
            P(),
            P(),
            P(),
            P(),
            P(),
            P(("band", "strip")),
            P(("band", "strip"), None),
            P(("band", "strip")),
            P(("band", "strip"), None),
            P(("band", "strip"), None),
        ),
        out_specs=(P("band", "strip", None), P(("band", "strip")), P()),
        check_vma=False,
    )
```

```python
import math

import jax
import jax.numpy as jnp
from jax import lax
from jax.experimental import pallas as pl
from jax.experimental.pallas import tpu as pltpu
from jax.sharding import PartitionSpec as P

HEADS = 8
EPS = 1e-06
TAU = 12.0
BF = jnp.bfloat16
F32 = jnp.float32
LOG2E = math.log2(math.e)
VMEM_ROW = 24 * 1024 * 1024
VMEM_COL = 36 * 1024 * 1024
VMEM_SMALL = 8 * 1024 * 1024


def _dot(a, b):
    return jnp.dot(a, b, preferred_element_type=F32)


def _dot_t(a, b):
    return lax.dot_general(a, b, (((1,), (1,)), ((), ())), preferred_element_type=F32)


def _norm(x, gain):
    return x * lax.rsqrt(jnp.mean(x * x, axis=-1, keepdims=True) + EPS) * gain


def _first_half(shape):
    return lax.broadcasted_iota(jnp.int32, shape, 1) % 128 < 64


def _segments():
    a, b = (lax.broadcasted_iota(jnp.int32, (256, 256), i) // 64 for i in (0, 1))
    return jnp.where(a == b, 1.0 / 64, 0.0).astype(BF)


def _turn(back):
    a, b = (lax.broadcasted_iota(jnp.int32, (256, 256), 1 - i if back else i) for i in (0, 1))
    return jnp.where(a == b % 8 * 32 + b // 8, 1.0, 0.0).astype(BF)


def _project(normed, wqkv_ref, seg, rows, q_s, k0_s, k1_s, v0_s, v1_s):
    half = 256
    even = _first_half((normed.shape[0], half))
    zero = jnp.zeros((normed.shape[0], half), BF)
    one = jnp.ones((normed.shape[0], half), BF)
    for h in range(2):
        lanes = slice(h * half, (h + 1) * half)
        q = _dot(normed, wqkv_ref[:, h * half : (h + 1) * half])
        scale = lax.rsqrt(_dot((q * q).astype(BF), seg) + EPS)
        q_s[rows, lanes] = (q * (scale * (TAU / 64 * LOG2E))).astype(BF)
        k = _dot(normed, wqkv_ref[:, 512 + h * half : 512 + (h + 1) * half])
        scale = lax.rsqrt(_dot((k * k).astype(BF), seg) + EPS)
        k = (k * scale).astype(BF)
        k0_s[rows, lanes] = jnp.where(even, k, zero)
        k1_s[rows, lanes] = jnp.where(even, zero, k)
        v = _dot(normed, wqkv_ref[:, 1024 + h * half : 1024 + (h + 1) * half]).astype(BF)
        v0_s[rows, lanes] = jnp.where(even, v, one)
        v1_s[rows, lanes] = jnp.where(even, one, v)


def _pair(q, k0, k1, v0, v1):
    o0 = _dot(jnp.exp2(_dot_t(q, k0)).astype(BF), v0)
    o1 = _dot(jnp.exp2(_dot_t(q, k1)).astype(BF), v1)
    even = _first_half(o0.shape)
    total = pltpu.roll(jnp.where(even, o1, o0), 64, 1)
    return (jnp.where(even, o0, o1) / total).astype(BF)


def _row_kernel(
    x_ref, g_ref, wqkv_any, wo_any, out_any, wqkv_s, wo_s, out_s, q_s, k0_s, k1_s, v0_s, v1_s, c_s, sems
):
    wqkv_copy = pltpu.make_async_copy(wqkv_any, wqkv_s, sems.at[0])
    wo_copy = pltpu.make_async_copy(wo_any, wo_s, sems.at[1])
    wqkv_copy.start()
    wo_copy.start()
    tok, blk = 1024, 256
    gain = g_ref[...]
    seg = _segments()
    wqkv_copy.wait()
    for t in range(tok // blk):
        x = x_ref[8 * t : 8 * t + 8].reshape(blk, 512).astype(F32)
        _project(
            _norm(x, gain).astype(BF), wqkv_s, seg, slice(t * blk, (t + 1) * blk), q_s, k0_s, k1_s, v0_s, v1_s
        )
    for p in range(4):
        lanes = slice(p * 128, (p + 1) * 128)
        k0, k1, v0, v1 = k0_s[:, lanes], k1_s[:, lanes], v0_s[:, lanes], v1_s[:, lanes]
        for t in range(tok // blk):
            rows = slice(t * blk, (t + 1) * blk)
            c_s[rows, lanes] = _pair(q_s[rows, lanes], k0, k1, v0, v1)
    wo_copy.wait()
    sent = []
    for t in range(tok // blk):
        x = x_ref[8 * t : 8 * t + 8].reshape(blk, 512).astype(F32)
        y = (x + _dot(c_s[t * blk : (t + 1) * blk, :], wo_s[...])).astype(BF).reshape(8, 4, 8, 512)
        for b in range(4):
            out_s[b, 8 * t : 8 * t + 8] = y[:, b]
        part = slice(8 * t, 8 * t + 8)
        sent.append(pltpu.make_async_copy(out_s.at[:, part], out_any.at[:, part], sems.at[2 + t]))
        sent[-1].start()
    for copy in sent:
        copy.wait()


def _rank(named):
    before = lax.broadcasted_iota(jnp.int32, (128, 128), 0) < lax.broadcasted_iota(jnp.int32, (128, 128), 1)
    return _dot(named.astype(F32).astype(BF), before.astype(F32).astype(BF)).astype(jnp.int32)


def _project_columns(x_ref, gain, apart, seg, wqkv_s, t_s, outs, wait):
    for t in range(4):
        x = x_ref[32 * t : 32 * t + 32].reshape(256, 512).astype(F32)
        normed = _dot(apart, _norm(x, gain).astype(BF)).astype(BF)
        for c in range(8):
            at = c * 128 + t * 32
            t_s[at : at + 32, :] = normed[32 * c : 32 * c + 32]
    wait()
    for t in range(4):
        rows = slice(t * 256, (t + 1) * 256)
        _project(t_s[rows, :], wqkv_s, seg, rows, *outs)


def _early_kernel(
    x_ref, g_ref, wqkv_any, listed_ref, me_ref, q_ref, k0_ref, k1_ref, v0_ref, v1_ref, note_ref, wqkv_s, t_s, sem
):
    wqkv_copy = pltpu.make_async_copy(wqkv_any, wqkv_s, sem)
    wqkv_copy.start()
    outs = (q_ref, k0_ref, k1_ref, v0_ref, v1_ref)
    band = me_ref[0]
    lane = lax.broadcasted_iota(jnp.int32, (128, 128), 1)
    for d in range(4):
        lister = lax.rem(band + d, 4)
        cell, owner, cap = (listed_ref[i, pl.ds(lister, 1), :] for i in range(3))
        named = lax.broadcasted_iota(jnp.int32, (128, 128), 0) == owner
        rank = _rank(named)
        home = (cell % 32) // 8
        token = jnp.where(home == band, (cell // 32) * 8 + cell % 8 + 1, 0)
        for m in range(2):
            of = lambda v: jnp.sum(jnp.where(named & (rank == m), v, 0), axis=1, keepdims=True)
            note = jnp.where(lane == 0, of(home + 1), jnp.where(lane == 1, of(cap // 128), of(cap % 128)))
            k = 2 * d + m
            note_ref[128 * k : 128 * (k + 1), :] = jnp.where(lane == 3, of(token) - 1, note).astype(F32)
    _project_columns(x_ref, g_ref[...], _turn(False), _segments(), wqkv_s, t_s, outs, wqkv_copy.wait)


def _col_kernel(
    x0_ref, x1_ref, g_ref, q_any, k0_any, k1_any, v0_any, v1_any, note_any, wqkv_any, wo_any, me_ref,
    y0_any, y1_any, y2_any, y3_any, send_any,
    wqkv_s, wo_s, y_s, send_s, early_s, note_s, q_s, k0_s, k1_s, v0_s, v1_s, c_s, t_s, sems,
):
    wqkv_copy = pltpu.make_async_copy(wqkv_any, wqkv_s, sems.at[0])
    wo_copy = pltpu.make_async_copy(wo_any, wo_s, sems.at[1])
    wqkv_copy.start()
    then = [
        pltpu.make_async_copy(early, early_s.at[i], sems.at[10 + i])
        for i, early in enumerate((q_any, k0_any, k1_any, v0_any, v1_any))
    ]
    note_copy = pltpu.make_async_copy(note_any, note_s, sems.at[15])

    def wait():
        wqkv_copy.wait()
        for copy in (*then, wo_copy, note_copy):
            copy.start()

    band = me_ref[0]
    blk = 256
    together = _turn(True)
    late = (q_s, k0_s, k1_s, v0_s, v1_s)
    _project_columns(x1_ref, g_ref[...], _turn(False), _segments(), wqkv_s, t_s, late, wait)
    for copy in then:
        copy.wait()
    for c in range(8):
        rows = slice(c * 128, (c + 1) * 128)
        for p in range(4):
            lanes = slice(p * 128, (p + 1) * 128)
            c_s[c * blk : (c + 1) * blk, lanes] = _pair(
                *(jnp.concatenate([early_s[i, rows, lanes], late[i][rows, lanes]], axis=0) for i in range(5))
            )
    wo_copy.wait()
    sent = []
    for d, y_any in enumerate((y0_any, y1_any, y2_any, y3_any)):
        to = lax.rem(band + d, 4)
        for r, x_ref in enumerate((x0_ref, x1_ref)):
            context = [c_s[pl.ds(pl.multiple_of(c * 256 + r * 128 + to * 32, 32), 32), :] for c in range(8)]
            context = _dot(together, jnp.concatenate(context, axis=0)).astype(BF)
            x = x_ref[pl.ds(32 * to, 32)].reshape(blk, 512).astype(F32)
            y_s[d, r] = (x + _dot(context, wo_s[...])).astype(BF).reshape(32, 8, 512)
        sent.append(pltpu.make_async_copy(y_s.at[d], y_any, sems.at[2 + d]))
        sent[-1].start()
    lane = lax.broadcasted_iota(jnp.int32, (128, 128), 1)
    token = lax.broadcasted_iota(jnp.int32, (128, 512), 1).astype(F32)
    note_copy.wait()
    for d in range(4):
        y = y_s[d].reshape(512, 512)
        for m in range(2):
            k = 2 * d + m
            rows = slice(128 * k, 128 * (k + 1))
            note = note_s[rows, :]
            at = note[:, 3:4]
            feature = _dot(jnp.where(token == at, 1.0, 0.0).astype(BF), y)
            t_s[rows, 128:] = feature[:, 128:].astype(BF)
            t_s[rows, :128] = jnp.where(at < 0, jnp.where(lane < 3, note, 0.0), feature[:, :128]).astype(BF)
    for g in range(4):
        features = [t_s[128 * k + 32 * g : 128 * k + 32 * g + 32, :] for k in range(8)]
        features = _dot(together, jnp.concatenate(features, axis=0))
        part = slice(32 * g, 32 * g + 32)
        send_s[part] = features.astype(BF).reshape(32, 8, 512)
        sent.append(pltpu.make_async_copy(send_s.at[part], send_any.at[part], sems.at[6 + g]))
        sent[-1].start()
    for copy in sent:
        copy.wait()


def _near(*arrays):
    return [pltpu.with_memory_space_constraint(a, pltpu.VMEM) for a in arrays]


def _far(*arrays):
    return [pltpu.with_memory_space_constraint(a, pltpu.HBM) for a in arrays]


VM = pl.BlockSpec(memory_space=pltpu.VMEM)
SM = pl.BlockSpec(memory_space=pltpu.SMEM)
ANY = pl.BlockSpec(memory_space=pl.ANY)


def _half_kernel(x_ref, out_ref):
    out_ref[...] = x_ref[...]


def second_half(x):
    block = (8, 32, 512)
    return pl.pallas_call(
        _half_kernel,
        grid=(4,),
        out_shape=pltpu.HBM((32, 32, 512), BF),
        in_specs=[pl.BlockSpec(block, lambda i: (i + 4, 0, 0))],
        out_specs=pl.BlockSpec(block, lambda i: (i, 0, 0)),
        compiler_params=pltpu.CompilerParams(vmem_limit_bytes=VMEM_SMALL),
        cost_estimate=pl.CostEstimate(flops=0, bytes_accessed=2_000_000, transcendentals=0),
        name="second_half",
    )(*_far(x))


def row_layer(x, gain, wqkv, wo):
    tokens = pltpu.VMEM((1024, 512), BF)
    return pl.pallas_call(
        _row_kernel,
        out_shape=pltpu.HBM((4, 32, 8, 512), BF),
        in_specs=[VM] * 2 + [ANY] * 2,
        out_specs=ANY,
        scratch_shapes=[pltpu.VMEM((512, 1536), BF), pltpu.VMEM((512, 512), BF), pltpu.VMEM((4, 32, 8, 512), BF)]
        + [tokens] * 6
        + [pltpu.SemaphoreType.DMA((6,))],
        compiler_params=pltpu.CompilerParams(vmem_limit_bytes=VMEM_ROW),
        cost_estimate=pl.CostEstimate(flops=12_000_000_000, bytes_accessed=4_000_000, transcendentals=8_000_000),
        name="row_layer",
    )(*_near(x), gain, *_far(wqkv, wo))


def early_columns(x0, gain, wqkv, listed, me):
    return pl.pallas_call(
        _early_kernel,
        out_shape=(pltpu.HBM((1024, 512), BF),) * 5 + (pltpu.HBM((1024, 128), F32),),
        in_specs=[VM] * 2 + [ANY, VM, SM],
        out_specs=(VM,) * 6,
        scratch_shapes=[pltpu.VMEM((512, 1536), BF), pltpu.VMEM((1024, 512), BF), pltpu.SemaphoreType.DMA],
        compiler_params=pltpu.CompilerParams(vmem_limit_bytes=VMEM_ROW),
        cost_estimate=pl.CostEstimate(flops=4_000_000_000, bytes_accessed=3_000_000, transcendentals=1_000_000),
        name="early_columns",
    )(*_near(x0), gain, *_far(wqkv), *_near(listed), me)


def col_layer(x0, x1, gain, early, wqkv, wo, me):
    tokens = pltpu.VMEM((1024, 512), BF)
    return pl.pallas_call(
        _col_kernel,
        out_shape=(pltpu.HBM((2, 32, 8, 512), BF),) * 4 + (pltpu.HBM((128, 8, 512), BF),),
        in_specs=[VM] * 3 + [ANY] * 8 + [SM],
        out_specs=(ANY,) * 5,
        scratch_shapes=[
            pltpu.VMEM((512, 1536), BF),
            pltpu.VMEM((512, 512), BF),
            pltpu.VMEM((4, 2, 32, 8, 512), BF),
            pltpu.VMEM((128, 8, 512), BF),
            pltpu.VMEM((5, 1024, 512), BF),
            pltpu.VMEM((1024, 128), F32),
        ]
        + [tokens] * 5
        + [pltpu.VMEM((2048, 512), BF), tokens]
        + [pltpu.SemaphoreType.DMA((16,))],
        compiler_params=pltpu.CompilerParams(vmem_limit_bytes=VMEM_COL),
        cost_estimate=pl.CostEstimate(flops=12_000_000_000, bytes_accessed=9_000_000, transcendentals=4_000_000),
        name="col_layer",
    )(*_near(x0, x1), gain, *_far(*early, wqkv, wo), me)


def _decode_kernel(f_ref, w1_any, w2_ref, out_ref, w1_s, logit_s, sem):
    w1_copy = pltpu.make_async_copy(w1_any, w1_s, sem)
    w1_copy.start()
    w2 = jnp.broadcast_to(w2_ref[...], (128, 512))
    note = lax.broadcasted_iota(jnp.int32, (256, 128), 1) < 3
    w1_copy.wait()
    for t in range(4):
        feats = f_ref[32 * t : 32 * t + 32].reshape(256, 512)
        hidden = jax.nn.gelu(_dot(feats, w1_s[...])).astype(BF)
        logit_s[t * 256 : (t + 1) * 256, :] = jnp.where(note, feats[:, :128].astype(F32), _dot_t(hidden, w2))
    lane = lax.broadcasted_iota(jnp.int32, (32, 128), 1)
    slots = [logit_s[pl.ds(k, 128, stride=8), :] for k in range(8)]
    total = jnp.zeros((1, 128), F32)
    found = []
    for b in range(4):
        for m in range(2):
            heard = [slots[2 * ((b - h) % 4) + m][32 * h : 32 * h + 32] for h in range(4)]
            logit = jnp.zeros((32, 128), F32)
            cap = jnp.zeros((32, 1), F32)
            for h in range(4):
                others = [heard[o] for o in range(4) if o != h]
                agree = [o[:, 0:1] == h + 1 for o in others]
                here = agree[0] & agree[1] & agree[2]
                logit = jnp.where(here, heard[h], logit)
                cap = jnp.where(here, others[0][:, 1:2] * 128 + others[0][:, 2:3], cap)
            value = jnp.maximum(logit, 0.0) + jnp.log1p(jnp.exp(-jnp.abs(logit)))
            found.append(value)
            total = total + jnp.sum(value * (cap * 0.001), axis=0, keepdims=True)
    for b in range(4):
        rows = jnp.where(lane == 3, found[2 * b], jnp.where(lane == 4, found[2 * b + 1], total))
        out_ref[32 * b : 32 * b + 32, :] = rows


def decode(features, w1, w2):
    return pl.pallas_call(
        _decode_kernel,
        out_shape=jax.ShapeDtypeStruct((128, 128), F32),
        in_specs=[VM, ANY, VM],
        out_specs=VM,
        scratch_shapes=[pltpu.VMEM((512, 512), BF), pltpu.VMEM((1024, 128), F32), pltpu.SemaphoreType.DMA],
        compiler_params=pltpu.CompilerParams(vmem_limit_bytes=VMEM_SMALL),
        cost_estimate=pl.CostEstimate(flops=600_000_000, bytes_accessed=2_000_000, transcendentals=600_000),
        name="decode",
    )(*_near(features), *_far(w1), w2)


def _power_kernel(back_ref, listed_ref, me_ref, power_ref, fleet_ref):
    back = back_ref[...]
    band = me_ref[0]
    named = lax.broadcasted_iota(jnp.int32, (128, 128), 0) == listed_ref[1, pl.ds(band, 1), :]
    rank = _rank(named)
    value = jnp.where(named, jnp.where(rank == 0, back[:, 3:4], back[:, 4:5]), 0.0)
    kilowatts = listed_ref[2, pl.ds(band, 1), :].astype(F32)
    power_ref[...] = kilowatts * 0.001 * jnp.sum(value, axis=0, keepdims=True)
    fleet_ref[...] = jnp.sum(back[:, 5:6], axis=0, keepdims=True) / 16384.0


def power(back, listed, me):
    return pl.pallas_call(
        _power_kernel,
        out_shape=(jax.ShapeDtypeStruct((1, 128), F32), jax.ShapeDtypeStruct((1, 1), F32)),
        in_specs=[VM, VM, SM],
        out_specs=(VM, VM),
        name="plant_power",
    )(*_near(back, listed), me)


def _assemble_kernel(p0_ref, p1_ref, p2_ref, p3_ref, me_ref, out_any, sems):
    copies = []
    for d, p_ref in enumerate((p0_ref, p1_ref, p2_ref, p3_ref)):
        place = lax.rem(me_ref[0] + 4 - d, 4)
        copies.append(pltpu.make_async_copy(p_ref, out_any.at[:, place], sems.at[d]))
        copies[-1].start()
    for copy in copies:
        copy.wait()


def assemble(parts, me):
    return pl.pallas_call(
        _assemble_kernel,
        out_shape=pltpu.HBM((64, 4, 8, 512), BF),
        in_specs=[VM] * 4 + [SM],
        out_specs=ANY,
        scratch_shapes=[pltpu.SemaphoreType.DMA((4,))],
        compiler_params=pltpu.CompilerParams(vmem_limit_bytes=VMEM_SMALL),
        cost_estimate=pl.CostEstimate(flops=0, bytes_accessed=4_000_000, transcendentals=0),
        name="assemble",
    )(*_near(*parts), me)


def body(
    cloud_field, row_gain, row_qkv, row_out, col_gain, col_qkv, col_out,
    plant_cell, plant_decoder_device, plant_capacity, decode_first, decode_second,
):
    everyone = ("band", "strip")
    a2a = lambda x, axis: lax.all_to_all(x, axis, split_axis=0, concat_axis=0, tiled=True)
    me = jnp.stack([lax.axis_index("band"), lax.axis_index("strip")]).astype(jnp.int32)
    listed = jnp.stack([plant_cell, plant_decoder_device[:, 0], plant_capacity])
    listed = lax.all_gather(listed, "band").transpose(1, 0, 2)

    second = second_half(cloud_field)
    second, first, listed = lax.optimization_barrier((second, a2a(cloud_field[:32], "strip"), listed))
    second = a2a(second, "strip")
    row_args = (row_gain.reshape(1, 512), row_qkv, row_out)
    first = a2a(row_layer(first, *row_args).reshape(128, 8, 512), everyone)
    second = a2a(row_layer(second, *row_args).reshape(128, 8, 512), everyone)
    gain = col_gain.reshape(1, 512)
    early = early_columns(first, gain, col_qkv, listed, me)
    *columns, features = col_layer(first, second, gain, early, col_qkv, col_out, me)
    features = a2a(features, everyone)
    columns = [c.reshape(64, 8, 512) for c in columns]
    parts = columns[:1] + [
        lax.ppermute(columns[d], "band", [(i, (i + d) % 4) for i in range(4)]) for d in (1, 2, 3)
    ]
    final_field = assemble(parts, me).reshape(64, 32, 512)
    payload = decode(features, decode_first, decode_second)
    back = a2a(payload.reshape(128, 1, 128), everyone).reshape(128, 128)
    plant_power, fleet = power(back, listed, me)
    return (final_field, plant_power.reshape(128), fleet.reshape(()))


def solution(mesh):
    return jax.shard_map(
        body,
        mesh=mesh,
        in_specs=(
            P("band", "strip", None),
            P(),
            P(),
            P(),
            P(),
            P(),
            P(),
            P(("band", "strip")),
            P(("band", "strip"), None),
            P(("band", "strip")),
            P(("band", "strip"), None),
            P(("band", "strip"), None),
        ),
        out_specs=(P("band", "strip", None), P(("band", "strip")), P()),
        check_vma=False,
    )
```
